256 devices in a mesh: site: 4 (over y), blk: 64 (over z, x, core).
Axes of the slice: x: 4, y: 4, z: 8, core: 2. Of those that a mesh axis runs over, the one named last changes fastest.
Arguments:
- sgt: bfloat16 [4, 2, 6, 2, 8192, 1024], P('site', None, None, None, 'blk'), may hold values from -6 to 6
- mechanism: float32 [6, 8192], P(None, 'blk'), may hold values from -2.5 to 2.5
- slip_fields: float32 [256, 3, 8192], P('blk', None, 'site'), may hold values from 0 to 20, as said below
- rupture_start: int32 [256], replicated, may hold values from 0 to 63, as said below
- point_count: int32 [256], replicated, may hold values from 32 to 2048, as said below
- owner_order: int32 [256], replicated, may hold values from 0 to 255, as said below
Outputs:
- spectral_accel: float32 [4, 256, 88], P('site', 'blk')
The draws below stay inside these ranges and needn't reach their ends.
Inputs may be any that keep to these rules, and one draw needn't show every extreme that they name: `point_count`: each variation's points lie within the fault. rupture_start[v] + ceil(point_count[v] / 128) <= 64. `owner_order`: a permutation; the variations held in the 4 slots j of one owner (equal j // 4) touch disjoint sets of fault blocks. `slip_fields`: channel 0 (slip) lies in 0.2 to 2, channel 1 (onset) in 0 to 20, channel 2 (rise time) in 0.05 to 0.5.
All inputs are finite; a program needn't handle non-finite values.
Results may differ from the reference program's by a relative error of at most 0.00084.
Values sent between devices are 32-bit elements; how exact they have to be, the bound alone decides.
A program may use at most 128 MiB of HBM per device.

```python
import jax
import jax.numpy as jnp
from jax import lax

FREQ = 1024
PERIODS = 44
BLK_PTS = 128
VAR_DEV = 4
SITES = 4
BLOCKS = 64
NPTS = 8192
VARS = 256


def rupture_layout(key):
    perm_key, seg_key, power_key, base_key, pick_key, place_key = jax.random.split(key, 6)
    order = jax.random.permutation(perm_key, VARS).astype(jnp.int32)
    seg_blocks = BLOCKS // VAR_DEV
    seg_pts = seg_blocks * BLK_PTS
    lowest = max(1, min(32, seg_pts // 4))
    owner_keys = jax.random.split(seg_key, BLOCKS)
    segments = jax.vmap(lambda k: jax.random.permutation(k, VAR_DEV))(owner_keys).reshape(VARS).astype(jnp.int32)
    levels = max(1, (seg_pts // lowest).bit_length())
    power = jax.random.randint(power_key, (VARS,), 0, levels)
    base = jax.random.randint(base_key, (VARS,), lowest, 2 * lowest + 1)
    counts = jnp.minimum(seg_pts, jnp.left_shift(jnp.ones_like(power), power) * base)
    chosen = jax.random.randint(pick_key, (), 0, VARS)
    counts = jnp.where(jnp.arange(VARS) == chosen, seg_pts, counts).astype(jnp.int32)
    span = (counts + BLK_PTS - 1) // BLK_PTS
    starts = (segments * seg_blocks + jax.random.randint(place_key, (VARS,), 0, seg_blocks - span + 1)).astype(jnp.int32)
    var_counts = jnp.zeros((VARS,), jnp.int32).at[order].set(counts)
    var_starts = jnp.zeros((VARS,), jnp.int32).at[order].set(starts)
    return (order, var_counts, var_starts)


def draw_owner_order(key, part):
    return rupture_layout(key)[0]


def draw_point_count(key, part):
    return rupture_layout(key)[1]


def draw_rupture_start(key, part):
    return rupture_layout(key)[2]


def draw_slip_fields(key, part):
    key = jax.random.fold_in(key, 7)
    slip_key, onset_key, rise_key = jax.random.split(key, 3)
    slip_amp = jnp.exp(jax.random.uniform(slip_key, (VARS, NPTS), jnp.float32, jnp.log(0.2), jnp.log(2.0)))
    onset = jax.random.uniform(onset_key, (VARS, NPTS), jnp.float32, 0.0, 20.0)
    rise_time = jnp.exp(jax.random.uniform(rise_key, (VARS, NPTS), jnp.float32, jnp.log(0.05), jnp.log(0.5)))
    return jnp.stack([slip_amp, onset, rise_time], axis=1).astype(jnp.float32)


def shard_levels(own_key, extent, pieces, smallest, largest):
    gain, own = 1.0, jax.random.fold_in(own_key, 6)
    for position, blocks in pieces:
        heights = jnp.exp(jax.random.uniform(jax.random.fold_in(own, position), (blocks,), jnp.float32, smallest / len(pieces), largest / len(pieces)))
        gain = gain * jnp.repeat(heights, extent[position] // blocks).reshape([-1 if axis == position else 1 for axis in range(len(extent))])
    return gain


def noise(own_key, extent, width, bound, pieces=(), held_as=jnp.bfloat16):
    values = width * jax.random.normal(own_key, extent, jnp.float32)
    if pieces:
        values = values * shard_levels(own_key, extent, pieces, -0.22, 0.18)
    return jnp.clip(values, -bound, bound).astype(held_as)


def setup_inputs(seed: int = 0) -> dict:
    key_list = jax.random.split(jax.random.key(seed), 7)
    sgt = noise(key_list[0], (SITES, 2, 6, 2, NPTS, FREQ), 1.0, 6.0, ((0, 4), (4, 64)))
    mechanism = noise(key_list[1], (6, NPTS), 6 ** -0.5, 2.5, ((1, 64),), jnp.float32)
    slip_fields = draw_slip_fields(jax.random.fold_in(key_list[6], 71), 0)
    rupture_start = draw_rupture_start(jax.random.fold_in(key_list[6], 71), 0)
    point_count = draw_point_count(jax.random.fold_in(key_list[6], 71), 0)
    owner_order = draw_owner_order(jax.random.fold_in(key_list[6], 71), 0)
    return dict(sgt=sgt, mechanism=mechanism, slip_fields=slip_fields, rupture_start=rupture_start, point_count=point_count, owner_order=owner_order)


DT = 0.1
DAMPING = 0.05

def angular(freq_count):
    return 2.0 * jnp.pi * jnp.arange(freq_count, dtype=jnp.float32) / (2 * freq_count * DT)

def source_terms(slip_amp, onset, rise_time, active, omega):
    scaled = jnp.where(active, slip_amp, 0.0)[..., None] / jnp.sqrt(1.0 + (omega * rise_time[..., None]) ** 2)
    phase = omega * onset[..., None]
    return (scaled * jnp.cos(phase), scaled * jnp.sin(phase))

def contract(cosine_part, sine_part, w_real, w_imag):
    w_real = w_real.astype(jnp.float32)
    w_imag = w_imag.astype(jnp.float32)
    real_sum = lax.optimization_barrier(jnp.sum(cosine_part * w_real + sine_part * w_imag, axis=-2))
    imag_sum = lax.optimization_barrier(jnp.sum(cosine_part * w_imag - sine_part * w_real, axis=-2))
    return jnp.stack([real_sum, imag_sum], axis=-2)

def dft_tables(freq_count):
    samples = 2 * freq_count
    freq_ids = jnp.arange(freq_count, dtype=jnp.int32)
    time_ids = jnp.arange(samples, dtype=jnp.int32)
    product = freq_ids[:, None] * time_ids[None, :] % samples
    angle = 2.0 * jnp.pi * product.astype(jnp.float32) / samples
    factor = jnp.where(freq_ids == 0, 1.0, 2.0).astype(jnp.float32) / freq_count
    return (factor[:, None] * jnp.cos(angle), factor[:, None] * jnp.sin(angle))

def oscillator_peaks(spectra, omega):
    freq_count = spectra.shape[-1]
    steps = jnp.arange(PERIODS, dtype=jnp.float32) / (PERIODS - 1)
    natural = 2.0 * jnp.pi / (0.2 * 50.0 ** steps)
    stiffness = natural[:, None] ** 2 - omega[None, :] ** 2
    friction = 2.0 * DAMPING * natural[:, None] * omega[None, :]
    gain_factor = natural[:, None] ** 2 / (stiffness ** 2 + friction ** 2)
    real_part = spectra[:, :, 0, None, :]
    imag_part = spectra[:, :, 1, None, :]
    resp_real = gain_factor * (real_part * stiffness + imag_part * friction)
    resp_imag = gain_factor * (imag_part * stiffness - real_part * friction)
    cosine, sine = dft_tables(freq_count)
    series = jnp.dot(resp_real.reshape(-1, freq_count), cosine, precision=lax.Precision.HIGHEST, preferred_element_type=jnp.float32)
    series = series - jnp.dot(resp_imag.reshape(-1, freq_count), sine, precision=lax.Precision.HIGHEST, preferred_element_type=jnp.float32)
    return lax.optimization_barrier(jnp.max(jnp.abs(series), axis=1)).reshape(spectra.shape[0], 2 * PERIODS)

def reference(sgt, mechanism, slip_fields, rupture_start, point_count, owner_order):

    def site_weights(site_sgt):
        total = jnp.zeros((2, 2, NPTS, FREQ), jnp.float32)
        for component in range(6):
            total = total + mechanism[component][None, None, :, None] * site_sgt[:, component].astype(jnp.float32)
        return total.astype(jnp.bfloat16)
    weights = lax.map(site_weights, sgt)
    omega = angular(FREQ)

    def one_variation(variation):
        start = rupture_start[variation]
        count = point_count[variation]
        span = (count + BLK_PTS - 1) // BLK_PTS
        fields = slip_fields[variation]

        def add_block(index, total):
            first_point = ((start + index) * BLK_PTS).astype(jnp.int32)
            piece = lax.dynamic_slice_in_dim(weights, first_point, BLK_PTS, 3)
            local = lax.dynamic_slice_in_dim(fields, first_point, BLK_PTS, 1)
            point_index = index * BLK_PTS + jnp.arange(BLK_PTS, dtype=jnp.int32)
            cosine_part, sine_part = source_terms(local[0], local[1], local[2], point_index < count, omega)
            return total + contract(cosine_part, sine_part, piece[:, :, 0], piece[:, :, 1])
        return lax.fori_loop(0, span, add_block, jnp.zeros((SITES, 2, 2, FREQ), jnp.float32))
    spectra = lax.map(one_variation, jnp.arange(VARS, dtype=jnp.int32))
    slotted = jnp.transpose(spectra[owner_order], (1, 0, 2, 3, 4))
    return lax.map(lambda rows: oscillator_peaks(rows, omega), slotted)
```

```python
import functools

import jax
import jax.numpy as jnp
import ml_dtypes
import numpy as np
from jax import lax
from jax.experimental import pallas as pl
from jax.experimental.pallas import tpu as pltpu
from jax.sharding import PartitionSpec as P

MESH = pl.DeviceIdType.MESH
FREQ = 1024
PERIODS = 44
PAD_PERIODS = 48
PTS = 128
SITES = 4
NZ = 8
NJ = 8
OWNERS = NZ * NJ
CHUNKS = 4
STEPS = 16
ROWS = 8 * PAD_PERIODS
HALF = FREQ // 2
DT = 0.1
DAMPING = 0.05
TURNS = 1.0 / (2 * FREQ * DT)
F32 = jnp.float32
BF16 = jnp.bfloat16


def split_table(table):
    high = table.astype(ml_dtypes.bfloat16)
    low = (table - high.astype(np.float64)).astype(ml_dtypes.bfloat16)
    return high, low


def constant_tables():
    freq = np.arange(FREQ)
    omega = 2 * np.pi * freq * TURNS
    factor = np.where(freq == 0, 1.0, 2.0) / FREQ
    natural = 2 * np.pi / (0.2 * 50.0 ** (np.arange(PERIODS) / (PERIODS - 1)))
    stiffness = natural[:, None] ** 2 - omega[None] ** 2
    friction = 2 * DAMPING * natural[:, None] * omega[None]
    gain = factor[None] * natural[:, None] ** 2 / (stiffness**2 + friction**2)
    response = np.zeros((2, 2, PAD_PERIODS, HALF), np.float32)
    for parity in range(2):
        response[parity, 0, :PERIODS] = (gain * stiffness)[:, parity::2]
        response[parity, 1, :PERIODS] = (gain * friction)[:, parity::2]
    sample = np.arange(HALF)
    tables = np.zeros((2, 2, 2, HALF, HALF), ml_dtypes.bfloat16)
    for parity in range(2):
        ids = freq[parity::2]
        angle = 2 * np.pi * ((ids[:, None] * sample[None]) % (2 * FREQ)) / (2 * FREQ)
        tables[parity, 0, 0], tables[parity, 0, 1] = split_table(np.cos(angle))
        sine = np.sin(angle)
        if parity == 1:
            sine[:, 0] = np.where(np.arange(HALF) % 2 == 0, 1.0, -1.0)
        tables[parity, 1, 0], tables[parity, 1, 1] = split_table(sine)
    return response, tables


def place():
    y = lax.axis_index("site")
    b = lax.axis_index("blk")
    return y, b, lax.div(b, NJ), lax.rem(b, NJ)


def greet(peers):
    barrier = pltpu.get_barrier_semaphore()
    for peer in peers:
        pl.semaphore_signal(barrier, inc=1, device_id=peer, device_id_type=MESH)
    pl.semaphore_wait(barrier, len(peers))


def remote(src, dst, send, recv, peer):
    return pltpu.make_async_remote_copy(
        src_ref=src, dst_ref=dst, send_sem=send, recv_sem=recv, device_id=peer, device_id_type=MESH
    )


def slip_kernel(
    start_ref, count_ref, order_ref, slip_ref, out_ref, mine, fault, plane, block,
    send_a, recv_a, send_b, recv_b, send_c, recv_c, send_d, recv_d,
):
    y, b, z, j = place()
    y_peers = [(lax.rem(y + d, SITES), b) for d in range(1, SITES)]
    j_peers = [(y, z * NJ + lax.rem(j + d, NJ)) for d in range(1, NJ)]
    z_peers = [(y, lax.rem(z + d, NZ) * NJ + j) for d in range(1, NZ)]
    greet(y_peers + j_peers + z_peers)
    for v in range(4):
        for zz in range(2):
            for jj in range(NJ):
                at = (zz * NJ + jj) * PTS
                mine[v, zz, jj, 0:3, :] = slip_ref[v, :, at : at + PTS]
    copies = []
    for d, peer in enumerate(y_peers):
        copy = remote(mine.at[peer[0]], fault.at[pl.ds(2 * y, 2)], send_a.at[d], recv_a.at[d], peer)
        copy.start()
        copies.append(copy)
    fault[pl.ds(2 * y, 2)] = mine[y]
    for copy in copies:
        copy.wait()
    copies = []
    for d, peer in enumerate(j_peers):
        target = lax.rem(j + d + 1, NJ)
        copy = remote(fault.at[:, target], plane.at[j], send_b.at[d], recv_b.at[d], peer)
        copy.start()
        copies.append(copy)
    plane[j] = fault[:, j]
    for copy in copies:
        copy.wait()
    copies = []
    for d, peer in enumerate(z_peers):
        target = lax.rem(z + d + 1, NZ)
        copy = remote(plane.at[:, target], block.at[y, z], send_c.at[d], recv_c.at[d], peer)
        copy.start()
        copies.append(copy)
    block[y, z] = plane[:, z]
    for copy in copies:
        copy.wait()
    copies = []
    for d, peer in enumerate(y_peers):
        copy = remote(block.at[y], block.at[y], send_d.at[d], recv_d.at[d], peer)
        copy.start()
        copies.append(copy)
    for copy in copies:
        copy.wait()

    lane = lax.broadcasted_iota(jnp.int32, (1, PTS), 1)

    def select(row, carry):
        owner = lax.rem(row, NZ) * NJ + lax.div(row, NZ)
        chosen = jnp.int32(0)
        points = jnp.int32(0)
        for slot in range(4):
            v = order_ref[owner * 4 + slot]
            first = start_ref[v]
            count = count_ref[v]
            left = count - (b - first) * PTS
            live = (first <= b) & (left > 0)
            chosen = jnp.where(live, v, chosen)
            points = jnp.where(live, left, points)
        fields = block[chosen & 3, lax.shift_right_logical(chosen, 5), lax.shift_right_logical(chosen, 2) & 7]
        out_ref[0, pl.ds(row, 1), :] = jnp.where(lane < points, fields[0:1], 0.0)
        out_ref[1, pl.ds(row, 1), :] = fields[1:2]
        out_ref[2, pl.ds(row, 1), :] = fields[2:3]
        return carry

    lax.fori_loop(0, OWNERS, select, 0)


def exchange_slip(slip, start, count, order):
    dma = pltpu.SemaphoreType.DMA
    smem = pl.BlockSpec(memory_space=pltpu.SMEM)
    vmem = pl.BlockSpec(memory_space=pltpu.VMEM)
    return pl.pallas_call(
        slip_kernel,
        out_shape=jax.ShapeDtypeStruct((3, OWNERS, PTS), F32),
        in_specs=[smem, smem, smem, vmem],
        out_specs=vmem,
        scratch_shapes=[
            pltpu.VMEM((4, 2, NJ, 4, PTS), F32),
            pltpu.VMEM((NZ, NJ, 4, PTS), F32),
            pltpu.VMEM((NJ, NZ, 4, PTS), F32),
            pltpu.VMEM((4, NZ, NJ, 4, PTS), F32),
            dma((3,)), dma((3,)), dma((7,)), dma((7,)), dma((7,)), dma((7,)), dma((3,)), dma((3,)),
        ],
        compiler_params=pltpu.CompilerParams(collective_id=0, has_side_effects=True),
        name="slip_exchange",
    )(start, count, order, slip)


def weights_kernel(sgt_ref, mech_ref, out_ref, mech_wide):
    turned = jnp.transpose(jnp.concatenate([mech_ref[...], jnp.zeros((2, PTS), F32)], axis=0))
    for k in range(6):
        mech_wide[k] = jnp.broadcast_to(turned[:, k : k + 1], (PTS, PTS))

    def tile(step, carry):
        at = pl.multiple_of(step * PTS, PTS)
        for c in range(2):
            for part in range(2):
                total = mech_wide[0] * sgt_ref[0, c, 0, part, :, pl.ds(at, PTS)].astype(F32)
                for k in range(1, 6):
                    total = total + mech_wide[k] * sgt_ref[0, c, k, part, :, pl.ds(at, PTS)].astype(F32)
                turned = jnp.transpose(total)
                rows = at * 4 + 2 * c
                if part == 0:
                    out_ref[0, pl.ds(rows, PTS, stride=4), :] = turned
                    out_ref[1, pl.ds(rows + 1, PTS, stride=4), :] = -turned
                else:
                    out_ref[1, pl.ds(rows, PTS, stride=4), :] = turned
                    out_ref[0, pl.ds(rows + 1, PTS, stride=4), :] = turned
        return carry

    lax.fori_loop(0, FREQ // PTS, tile, 0)


def make_weights(sgt, mechanism):
    vmem = pl.BlockSpec(memory_space=pltpu.VMEM)
    return pl.pallas_call(
        weights_kernel,
        out_shape=jax.ShapeDtypeStruct((2, FREQ * 4, PTS), F32),
        in_specs=[vmem, vmem],
        out_specs=vmem,
        scratch_shapes=[pltpu.VMEM((6, PTS, PTS), F32)],
        compiler_params=pltpu.CompilerParams(vmem_limit_bytes=32 * 2**20),
        name="weights",
    )(sgt, mechanism)


def circle(turns):
    half = (turns - jnp.floor(turns + 0.5)) * jnp.float32(np.pi)
    sq = half * half
    sine = jnp.float32(1.0 / 6227020800)
    for sign, power in ((-1, 39916800), (1, 362880), (-1, 5040), (1, 120), (-1, 6)):
        sine = sine * sq + jnp.float32(sign / power)
    sine = half + half * sq * sine
    cosine = jnp.float32(-1.0 / 87178291200)
    for sign, power in ((1, 479001600), (-1, 3628800), (1, 40320), (-1, 720), (1, 24), (-1, 2)):
        cosine = cosine * sq + jnp.float32(sign / power)
    cosine = cosine * sq + 1.0
    return 1.0 - 2.0 * sine * sine, 2.0 * sine * cosine


def spectra_kernel(fields_ref, weights_ref, out_ref, state, sources, sums):
    amp = fields_ref[0]
    turns = fields_ref[1] * jnp.float32(TURNS)
    rise = fields_ref[2] * jnp.float32(2 * np.pi * TURNS)
    one_c, one_s = circle(turns)
    state[0] = amp
    state[1] = jnp.zeros_like(amp)
    state[2] = amp * one_c
    state[3] = amp * one_s
    step_c, step_s = circle(turns * 2.0)
    state[4] = step_c
    state[5] = step_s
    state[8] = 2.0 * step_c
    jump_c, jump_s = circle(turns * jnp.float32(2 * STEPS))
    state[6] = jump_c
    state[7] = jump_s
    state[9] = rise * rise

    def run(turn, carry):
        base = turn * (2 * STEPS)
        for pair in range(OWNERS // 16):
            rows = slice(pair * 16, pair * 16 + 16)
            double = state[8, rows]
            rise_sq = state[9, rows]
            for parity in range(2):
                cos_now, sin_now = state[2 * parity, rows], state[2 * parity + 1, rows]
                step_c, step_s = state[4, rows], state[5, rows]
                jump_c, jump_s = state[6, rows], state[7, rows]
                state[2 * parity, rows] = cos_now * jump_c - sin_now * jump_s
                state[2 * parity + 1, rows] = sin_now * jump_c + cos_now * jump_s
                cos_next = cos_now * step_c - sin_now * step_s
                sin_next = sin_now * step_c + cos_now * step_s
                for i in range(STEPS):
                    freq = (base + (2 * i + parity)).astype(F32)
                    scale = lax.rsqrt(rise_sq * (freq * freq) + 1.0)
                    at = parity * OWNERS + pair * 16
                    sources[i, at : at + 16, 0:PTS] = (cos_now * scale).astype(BF16)
                    sources[i, at : at + 16, PTS:] = (sin_now * scale).astype(BF16)
                    if i < STEPS - 1:
                        cos_now, cos_next = cos_next, double * cos_next - cos_now
                        sin_now, sin_next = sin_next, double * sin_next - sin_now
        local = lax.rem(turn, 128 // STEPS) * STEPS
        for i in range(0, STEPS, 2):
            first = pl.multiple_of((turn * STEPS + i) * 8, 16)
            left = jnp.concatenate([weights_ref[0, pl.ds(first, 16)], weights_ref[1, pl.ds(first, 16)]], axis=1).astype(BF16)
            right = sources[i : i + 2].reshape(2 * PTS, 2 * PTS)
            product = lax.dot_general(left, right, (((1,), (1,)), ((), ())), preferred_element_type=F32)
            sums[pl.ds(local + i, 8, stride=128), :] = product[0:8, 0:128]
            sums[pl.ds(local + i + 1, 8, stride=128), :] = product[8:16, 128:256]
        return carry

    def chunk(h, carry):
        lax.fori_loop(h * (128 // STEPS), (h + 1) * (128 // STEPS), run, 0)
        for row in range(8):
            turned = jnp.transpose(sums[row * 128 : (row + 1) * 128, :])
            parity = row // 4
            out_ref[h, row] = turned[parity * OWNERS : (parity + 1) * OWNERS]
        return carry

    lax.fori_loop(0, CHUNKS, chunk, 0)


def partial_spectra(fields, weights):
    vmem = pl.BlockSpec(memory_space=pltpu.VMEM)
    return pl.pallas_call(
        spectra_kernel,
        out_shape=jax.ShapeDtypeStruct((CHUNKS, 8, OWNERS, 128), F32),
        in_specs=[vmem, vmem],
        out_specs=vmem,
        scratch_shapes=[
            pltpu.VMEM((10, OWNERS, PTS), F32),
            pltpu.VMEM((STEPS, 2 * OWNERS, 2 * PTS), BF16),
            pltpu.VMEM((8 * 128, 128), F32),
        ],
        compiler_params=pltpu.CompilerParams(vmem_limit_bytes=32 * 2**20),
        name="partial_spectra",
    )(fields, weights)


def peaks_kernel(
    start_ref, count_ref, order_ref, parts_ref, response_ref, table_ref, out_ref,
    arrived, summed, landed, limits, left, extra, best,
    send_a, recv_a, send_b, recv_b,
):
    y, b, z, j = place()
    j_peers = [(y, z * NJ + lax.rem(j + d, NJ)) for d in range(1, NJ)]
    z_peers = [(y, lax.rem(z + d, NZ) * NJ + j) for d in range(1, NZ)]
    greet(j_peers + z_peers)
    first_hop = []
    for h in range(CHUNKS):
        for d, peer in enumerate(j_peers):
            rows = pl.multiple_of(lax.rem(j + d + 1, NJ) * NZ, 8)
            copy = remote(
                parts_ref.at[h, :, pl.ds(rows, NZ), :], arrived.at[h, j],
                send_a.at[h, d], recv_a.at[h, d], peer,
            )
            copy.start()
            first_hop.append(copy)
    for h in range(CHUNKS):
        arrived[h, j] = parts_ref[h, :, pl.ds(pl.multiple_of(j * NZ, 8), NZ), :]

    def bounds(index, carry):
        slot, zz = lax.div(index, NZ), lax.rem(index, NZ)
        v = order_ref[(zz * NJ + j) * 4 + slot]
        first = start_ref[v]
        span = lax.shift_right_logical(count_ref[v] + (PTS - 1), 7)
        limits[0, pl.ds(index, 1), :] = jnp.full((1, 128), first, jnp.int32)
        limits[1, pl.ds(index, 1), :] = jnp.full((1, 128), first + span, jnp.int32)
        return carry

    lax.fori_loop(0, 4 * NZ, bounds, 0)

    second_hop = []
    for h in range(CHUNKS):
        for copy in first_hop[h * 7 : h * 7 + 7]:
            copy.wait()
        for slot in range(4):
            first = limits[0, slot * NZ : slot * NZ + NZ]
            last = limits[1, slot * NZ : slot * NZ + NZ]
            total = jnp.zeros((8, NZ, 128), F32)
            for src in range(NJ):
                at = z * NJ + src
                live = (first <= at) & (at < last)
                total = total + jnp.where(live[None], arrived[h, src], 0.0)
            for row in range(8):
                summed[h, pl.ds(slot * 8 + row, NZ, stride=32), :] = total[row]
        for d, peer in enumerate(z_peers):
            rows = pl.multiple_of(lax.rem(z + d + 1, NZ) * 32, 32)
            copy = remote(
                summed.at[h, pl.ds(rows, 32), :], landed.at[h, z], send_b.at[h, d], recv_b.at[h, d], peer
            )
            copy.start()
            second_hop.append(copy)
        landed[h, z] = summed[h, pl.ds(pl.multiple_of(z * 32, 32), 32), :]

    lane = lax.broadcasted_iota(jnp.int32, (1, 128), 1)
    sign = jnp.where(lax.rem(lane, 2) == 0, 1.0, -1.0).astype(F32)
    for h in range(CHUNKS):
        for copy in second_hop[h * 7 : h * 7 + 7]:
            copy.wait()
        total = landed[h, 0]
        for src in range(1, NZ):
            total = total + landed[h, src]
        cols = slice(h * 128, h * 128 + 128)
        for parity in range(2):
            stiff = response_ref[parity, 0, :, cols]
            friction = response_ref[parity, 1, :, cols]
            for slot in range(4):
                for c in range(2):
                    row = slot * 8 + parity * 4 + 2 * c
                    real, imag = total[row : row + 1], total[row + 1 : row + 2]
                    rows = slice((slot * 2 + c) * PAD_PERIODS, (slot * 2 + c + 1) * PAD_PERIODS)
                    for part, value in enumerate(
                        (real * stiff + imag * friction, imag * stiff - real * friction)
                    ):
                        high = value.astype(BF16)
                        left[parity, part, 0, rows, cols] = high
                        left[parity, part, 1, rows, cols] = (value - high.astype(F32)).astype(BF16)
                        if parity == 0 and part == 0:
                            if h == 0:
                                extra[rows, :] = value * sign
                            else:
                                extra[rows, :] += value * sign

    def series(parity, part, rows, cols):
        high, low = left[parity, part, 0, rows], left[parity, part, 1, rows]
        table_high, table_low = table_ref[parity, part, 0, :, cols], table_ref[parity, part, 1, :, cols]
        dot = functools.partial(jnp.dot, preferred_element_type=F32)
        return dot(high, table_high) + (dot(low, table_high) + dot(high, table_low))

    tile_rows = 2 * PAD_PERIODS

    def tile(index, carry):
        rows = pl.ds(pl.multiple_of(index * tile_rows, tile_rows), tile_rows)
        most = jnp.zeros((tile_rows, 128), F32)
        for col in range(HALF // 256):
            cols = slice(col * 256, col * 256 + 256)
            cos_even, cos_odd = series(0, 0, rows, cols), series(1, 0, rows, cols)
            sin_even, sin_odd = series(0, 1, rows, cols), series(1, 1, rows, cols)
            if col == 0:
                middle = jnp.abs(jnp.sum(extra[rows], axis=1, keepdims=True)) + jnp.abs(sin_odd[:, 0:1])
                most = jnp.maximum(most, middle)
                wide = lax.broadcasted_iota(jnp.int32, (1, 256), 1)
                sin_odd = jnp.where(wide == 0, 0.0, sin_odd)
            one = jnp.abs(cos_even + cos_odd) + jnp.abs(sin_even + sin_odd)
            two = jnp.abs(cos_even - cos_odd) + jnp.abs(sin_odd - sin_even)
            peak = jnp.maximum(one, two)
            most = jnp.maximum(most, jnp.maximum(peak[:, :128], peak[:, 128:]))
        best[rows] = most
        return carry

    lax.fori_loop(0, 4, tile, 0)
    for slot in range(4):
        pieces = []
        for c in range(2):
            at = (slot * 2 + c) * PAD_PERIODS
            turned = jnp.transpose(jnp.concatenate([best[at : at + PAD_PERIODS], jnp.zeros((128 - PAD_PERIODS, 128), F32)], axis=0))
            pieces.append(jnp.max(turned, axis=0, keepdims=True))
        moved = pltpu.roll(pieces[1], PERIODS, 1)
        row = jnp.where(lane < PERIODS, pieces[0], moved)
        out_ref[0, slot : slot + 1, :] = row[:, : 2 * PERIODS]


def owner_peaks(parts, start, count, order, response, tables):
    dma = pltpu.SemaphoreType.DMA
    smem = pl.BlockSpec(memory_space=pltpu.SMEM)
    vmem = pl.BlockSpec(memory_space=pltpu.VMEM)
    return pl.pallas_call(
        peaks_kernel,
        out_shape=jax.ShapeDtypeStruct((1, 4, 2 * PERIODS), F32),
        in_specs=[smem, smem, smem, vmem, vmem, vmem],
        out_specs=vmem,
        scratch_shapes=[
            pltpu.VMEM((CHUNKS, NJ, 8, NZ, 128), F32),
            pltpu.VMEM((CHUNKS, NZ * 32, 128), F32),
            pltpu.VMEM((CHUNKS, NZ, 32, 128), F32),
            pltpu.VMEM((2, 4 * NZ, 128), jnp.int32),
            pltpu.VMEM((2, 2, 2, ROWS, HALF), BF16),
            pltpu.VMEM((ROWS, 128), F32),
            pltpu.VMEM((ROWS, 128), F32),
            dma((CHUNKS, 7)), dma((CHUNKS, 7)), dma((CHUNKS, 7)), dma((CHUNKS, 7)),
        ],
        compiler_params=pltpu.CompilerParams(
            collective_id=1, has_side_effects=True, vmem_limit_bytes=40 * 2**20
        ),
        name="owner_peaks",
    )(start, count, order, parts, response, tables)


def solution(mesh):
    response, tables = constant_tables()

    def per_device(sgt, mechanism, slip_fields, rupture_start, point_count, owner_order):
        weights = make_weights(sgt, mechanism)
        fields = exchange_slip(slip_fields, rupture_start, point_count, owner_order)
        parts = partial_spectra(fields, weights)
        return owner_peaks(
            parts, rupture_start, point_count, owner_order, jnp.asarray(response), jnp.asarray(tables)
        )

    return jax.shard_map(
        per_device,
        mesh=mesh,
        in_specs=(
            P("site", None, None, None, "blk", None),
            P(None, "blk"),
            P("blk", None, "site"),
            P(),
            P(),
            P(),
        ),
        out_specs=P("site", "blk", None),
        check_vma=False,
    )
```

```python
import functools

import jax
import jax.numpy as jnp
import ml_dtypes
import numpy as np
from jax import lax
from jax.experimental import pallas as pl
from jax.experimental.pallas import tpu as pltpu
from jax.sharding import PartitionSpec as P

MESH = pl.DeviceIdType.MESH
FREQ = 1024
PERIODS = 44
PAD_PERIODS = 48
PTS = 128
SITES = 4
NZ = 8
NJ = 8
OWNERS = NZ * NJ
CHUNKS = 4
STEPS = 32
ROWS = 8 * PAD_PERIODS
HALF = FREQ // 2
DT = 0.1
DAMPING = 0.05
TURNS = 1.0 / (2 * FREQ * DT)
F32 = jnp.float32
BF16 = jnp.bfloat16


def split_table(table):
    high = table.astype(ml_dtypes.bfloat16)
    low = (table - high.astype(np.float64)).astype(ml_dtypes.bfloat16)
    return high, low


def constant_tables():
    freq = np.arange(FREQ)
    omega = 2 * np.pi * freq * TURNS
    factor = np.where(freq == 0, 1.0, 2.0) / FREQ
    natural = 2 * np.pi / (0.2 * 50.0 ** (np.arange(PERIODS) / (PERIODS - 1)))
    stiffness = natural[:, None] ** 2 - omega[None] ** 2
    friction = 2 * DAMPING * natural[:, None] * omega[None]
    number = np.where(freq == 0, 2.0**-10, freq)
    gain = factor[None] / number[None] * natural[:, None] ** 2 / (stiffness**2 + friction**2)
    response = np.zeros((2, 2, PAD_PERIODS, HALF), np.float32)
    for parity in range(2):
        response[parity, 0, :PERIODS] = (gain * stiffness)[:, parity::2]
        response[parity, 1, :PERIODS] = (gain * friction)[:, parity::2]
    sample = np.arange(HALF)
    tables = np.zeros((2, 2, 2, HALF, HALF), ml_dtypes.bfloat16)
    for parity in range(2):
        ids = freq[parity::2]
        angle = 2 * np.pi * ((ids[:, None] * sample[None]) % (2 * FREQ)) / (2 * FREQ)
        tables[parity, 0, 0], tables[parity, 0, 1] = split_table(np.cos(angle))
        sine = np.sin(angle)
        if parity == 1:
            sine[:, 0] = np.where(np.arange(HALF) % 2 == 0, 1.0, -1.0)
        tables[parity, 1, 0], tables[parity, 1, 1] = split_table(sine)
    return response, tables, (1.0 / number**2).astype(np.float32)


def place():
    y = lax.axis_index("site")
    b = lax.axis_index("blk")
    return y, b, lax.div(b, NJ), lax.rem(b, NJ)


def greet(peers):
    barrier = pltpu.get_barrier_semaphore()
    for peer in peers:
        pl.semaphore_signal(barrier, inc=1, device_id=peer, device_id_type=MESH)
    pl.semaphore_wait(barrier, len(peers))


def remote(src, dst, send, recv, peer):
    return pltpu.make_async_remote_copy(
        src_ref=src, dst_ref=dst, send_sem=send, recv_sem=recv, device_id=peer, device_id_type=MESH
    )


def fields_kernel(
    start_ref, count_ref, order_ref, slip_ref, mech_ref, sgt_ref,
    fields_ref, weights_ref, limits_ref,
    mine, plane, block, chosen, points, mech_wide, sgt,
    send_a, recv_a, send_b, recv_b, send_c, recv_c, load_sem,
):
    y, b, z, j = place()
    loads = [pltpu.make_async_copy(sgt_ref.at[0, c], sgt.at[c], load_sem.at[c]) for c in range(2)]
    for load in loads:
        load.start()
    y_peers = [(lax.rem(y + d, SITES), b) for d in range(1, SITES)]
    z_peers = [(y, lax.rem(z + d, NZ) * NJ + j) for d in range(1, NZ)]
    turns = [(dy, dj) for dj in range(NJ) for dy in range(SITES) if dy or dj]
    plane_peers = [(lax.rem(y + dy, SITES), z * NJ + lax.rem(j + dj, NJ)) for dy, dj in turns]
    greet(plane_peers + z_peers)
    for v in range(4):
        for zz in range(2):
            for jj in range(NJ):
                at = (zz * NJ + jj) * PTS
                for k in range(3):
                    mine[v, jj, zz, k] = slip_ref[k, v : v + 1, at : at + PTS]
    copies = []
    for d, peer in enumerate(plane_peers):
        copy = remote(
            mine.at[peer[0], lax.rem(peer[1], NJ)], plane.at[j, pl.ds(2 * y, 2)], send_a.at[d], recv_a.at[d], peer
        )
        copy.start()
        copies.append(copy)
    plane[j, pl.ds(2 * y, 2)] = mine[y, j]

    turned = jnp.transpose(jnp.concatenate([mech_ref[...], jnp.zeros((2, PTS), F32)], axis=0))
    for k in range(6):
        mech_wide[k] = jnp.broadcast_to(turned[:, k : k + 1], (PTS, PTS))

    def weights_of(c):
        def tile(step, carry):
            at = pl.multiple_of(step * PTS, PTS)
            for part in range(2):
                total = mech_wide[0] * sgt[c, 0, part, :, pl.ds(at, PTS)].astype(F32)
                for k in range(1, 6):
                    total = total + mech_wide[k] * sgt[c, k, part, :, pl.ds(at, PTS)].astype(F32)
                turned = jnp.transpose(total)
                rows = at * 4 + 2 * c
                weights_ref[part, pl.ds(rows, PTS, stride=4), :] = turned
                weights_ref[1 - part, pl.ds(rows + 1, PTS, stride=4), :] = turned if part else -turned
            return carry

        lax.fori_loop(0, FREQ // PTS, tile, 0)

    loads[0].wait()
    weights_of(0)
    for copy in copies:
        copy.wait()
    copies = []
    for d, peer in enumerate(z_peers):
        target = lax.rem(z + d + 1, NZ)
        copy = remote(plane.at[:, target], block.at[y, z], send_b.at[d], recv_b.at[d], peer)
        copy.start()
        copies.append(copy)
    block[y, z] = plane[:, z]
    spread = []

    def forward(turn, row):
        for d, peer in enumerate(y_peers):
            copy = remote(block.at[y, row], block.at[y, row], send_c.at[turn, d], recv_c.at[turn, d], peer)
            copy.start()
            spread.append(copy)

    forward(0, z)

    def choose(row, carry):
        owner = lax.rem(row, NZ) * NJ + lax.div(row, NZ)
        best = jnp.int32(0)
        active = jnp.int32(0)
        for slot in range(4):
            v = order_ref[owner * 4 + slot]
            first = start_ref[v]
            remaining = count_ref[v] - (b - first) * PTS
            live = (first <= b) & (remaining > 0)
            best = jnp.where(live, v, best)
            active = jnp.where(live, remaining, active)
        chosen[row] = best
        points[row] = active
        return carry

    lax.fori_loop(0, OWNERS, choose, 0)
    for d, copy in enumerate(copies):
        copy.wait_recv()
        forward(d + 1, lax.rem(z + NZ - d - 1, NZ))

    def bounds(index, carry):
        slot, zz = lax.div(index, NZ), lax.rem(index, NZ)
        v = order_ref[(zz * NJ + j) * 4 + slot]
        first = start_ref[v]
        span = lax.shift_right_logical(count_ref[v] + (PTS - 1), 7)
        limits_ref[0, pl.ds(index, 1), :] = jnp.full((1, 128), first, jnp.int32)
        limits_ref[1, pl.ds(index, 1), :] = jnp.full((1, 128), first + span, jnp.int32)
        return carry

    lax.fori_loop(0, 4 * NZ, bounds, 0)
    loads[1].wait()
    weights_of(1)
    for copy in copies:
        copy.wait_send()
    for copy in spread:
        copy.wait()

    lane = lax.broadcasted_iota(jnp.int32, (1, PTS), 1)

    def select(row, carry):
        v = chosen[row]
        at = (v & 3, lax.shift_right_logical(v, 5), lax.shift_right_logical(v, 2) & 7)
        fields_ref[0, pl.ds(row, 1), :] = jnp.where(lane < points[row], block[at + (0,)], 0.0)
        fields_ref[1, pl.ds(row, 1), :] = block[at + (1,)]
        fields_ref[2, pl.ds(row, 1), :] = block[at + (2,)]
        return carry

    lax.fori_loop(0, OWNERS, select, 0)


def fields_and_weights(sgt, mechanism, slip, start, count, order):
    dma = pltpu.SemaphoreType.DMA
    smem = pl.BlockSpec(memory_space=pltpu.SMEM)
    vmem = pl.BlockSpec(memory_space=pltpu.VMEM)
    return pl.pallas_call(
        fields_kernel,
        out_shape=(
            jax.ShapeDtypeStruct((3, OWNERS, PTS), F32),
            jax.ShapeDtypeStruct((2, FREQ * 4, PTS), F32),
            jax.ShapeDtypeStruct((2, 4 * NZ, 128), jnp.int32),
        ),
        in_specs=[smem, smem, smem, vmem, vmem, pl.BlockSpec(memory_space=pl.ANY)],
        out_specs=(vmem, vmem, vmem),
        scratch_shapes=[
            pltpu.VMEM((4, NJ, 2, 3, 1, PTS), F32),
            pltpu.VMEM((NJ, NZ, 3, 1, PTS), F32),
            pltpu.VMEM((4, NZ, NJ, 3, 1, PTS), F32),
            pltpu.SMEM((OWNERS,), jnp.int32),
            pltpu.SMEM((OWNERS,), jnp.int32),
            pltpu.VMEM((6, PTS, PTS), F32),
            pltpu.VMEM((2, 6, 2, PTS, FREQ), BF16),
            dma((31,)), dma((31,)), dma((7,)), dma((7,)), dma((8, 3)), dma((8, 3)), dma((2,)),
        ],
        compiler_params=pltpu.CompilerParams(
            collective_id=0, has_side_effects=True, vmem_limit_bytes=40 * 2**20
        ),
        name="fields_and_weights",
    )(start, count, order, jnp.transpose(slip, (1, 0, 2)), mechanism, sgt)


def circle(turns):
    half = (turns - jnp.floor(turns + 0.5)) * jnp.float32(np.pi)
    sq = half * half
    sine = jnp.float32(1.0 / 6227020800)
    for sign, power in ((-1, 39916800), (1, 362880), (-1, 5040), (1, 120), (-1, 6)):
        sine = sine * sq + jnp.float32(sign / power)
    sine = half + half * sq * sine
    cosine = jnp.float32(-1.0 / 87178291200)
    for sign, power in ((1, 479001600), (-1, 3628800), (1, 40320), (-1, 720), (1, 24), (-1, 2)):
        cosine = cosine * sq + jnp.float32(sign / power)
    cosine = cosine * sq + 1.0
    return 1.0 - 2.0 * sine * sine, 2.0 * sine * cosine


def peaks_kernel(
    inverse_ref, fields_ref, weights_ref, limits_ref, response_ref, table_ref, out_ref,
    state, source_cos, source_sin, sums, parts, arrived, summed, landed, left, extra, total_series, best,
    send_a, recv_a, send_b, recv_b,
):
    y, b, z, j = place()
    j_peers = [(y, z * NJ + lax.rem(j + d, NJ)) for d in range(1, NJ)]
    z_peers = [(y, lax.rem(z + d, NZ) * NJ + j) for d in range(1, NZ)]
    barrier = pltpu.get_barrier_semaphore()
    for peer in j_peers + z_peers:
        pl.semaphore_signal(barrier, inc=1, device_id=peer, device_id_type=MESH)

    amp = fields_ref[0]
    turns = fields_ref[1] * jnp.float32(TURNS)
    rise = fields_ref[2] * jnp.float32(2 * np.pi * TURNS)
    one_c, one_s = circle(turns)
    state[0] = amp
    state[1] = jnp.zeros_like(amp)
    state[2] = amp * one_c
    state[3] = amp * one_s
    step_c, step_s = circle(turns * 2.0)
    state[4] = step_c
    state[5] = step_s
    state[8] = 2.0 * step_c
    jump_c, jump_s = circle(turns * jnp.float32(2 * STEPS))
    state[6] = jump_c
    state[7] = jump_s
    state[9] = rise * rise

    def run(turn, carry):
        base = turn * (2 * STEPS)
        for pair in range(OWNERS // 16):
            rows = slice(pair * 16, pair * 16 + 16)
            double = state[8, rows]
            rise_sq = state[9, rows]
            for parity in range(2):
                cos_now, sin_now = state[2 * parity, rows], state[2 * parity + 1, rows]
                step_c, step_s = state[4, rows], state[5, rows]
                jump_c, jump_s = state[6, rows], state[7, rows]
                state[2 * parity, rows] = cos_now * jump_c - sin_now * jump_s
                state[2 * parity + 1, rows] = sin_now * jump_c + cos_now * jump_s
                cos_next = cos_now * step_c - sin_now * step_s
                sin_next = sin_now * step_c + cos_now * step_s
                at = parity * OWNERS + pair * 16
                for i in range(STEPS):
                    scale = lax.rsqrt(rise_sq + inverse_ref[base + (2 * i + parity)])
                    source_cos[i, at : at + 16, :] = (cos_now * scale).astype(BF16)
                    source_sin[i, at : at + 16, :] = (sin_now * scale).astype(BF16)
                    if i < STEPS - 1:
                        cos_now, cos_next = cos_next, double * cos_next - cos_now
                        sin_now, sin_next = sin_next, double * sin_next - sin_now
        local = lax.rem(turn, 128 // STEPS) * STEPS
        for i in range(0, STEPS, 2):
            first = pl.multiple_of((turn * STEPS + i) * 8, 16)
            lhs = jnp.concatenate([weights_ref[0, pl.ds(first, 16)], weights_ref[1, pl.ds(first, 16)]], axis=1).astype(BF16)
            rhs = jnp.concatenate(
                [source_cos[i : i + 2].reshape(2 * PTS, PTS), source_sin[i : i + 2].reshape(2 * PTS, PTS)], axis=1
            )
            product = lax.dot_general(lhs, rhs, (((1,), (1,)), ((), ())), preferred_element_type=F32)
            sums[pl.ds(local + i, 8, stride=128), :] = product[0:8, 0:128]
            sums[pl.ds(local + i + 1, 8, stride=128), :] = product[8:16, 128:256]
        return carry

    def send_parts(h):
        for row in range(8):
            turned = jnp.transpose(sums[row * 128 : (row + 1) * 128, :])
            parity = row // 4
            parts[h, row] = turned[parity * OWNERS : (parity + 1) * OWNERS]
        copies = []
        for d, peer in enumerate(j_peers):
            rows = pl.multiple_of(lax.rem(j + d + 1, NJ) * NZ, 8)
            copy = remote(
                parts.at[h, :, pl.ds(rows, NZ), :], arrived.at[h, j], send_a.at[h, d], recv_a.at[h, d], peer
            )
            copy.start()
            copies.append(copy)
        arrived[h, j] = parts[h, :, pl.ds(pl.multiple_of(j * NZ, 8), NZ), :]
        return copies

    def send_sums(h, copies):
        for copy in copies:
            copy.wait()
        for slot in range(4):
            first = limits_ref[0, slot * NZ : slot * NZ + NZ]
            last = limits_ref[1, slot * NZ : slot * NZ + NZ]
            total = jnp.zeros((8, NZ, 128), F32)
            for src in range(NJ):
                at = z * NJ + src
                live = (first <= at) & (at < last)
                total = total + jnp.where(live[None], arrived[h, src], 0.0)
            for row in range(8):
                summed[h, pl.ds(slot * 8 + row, NZ, stride=32), :] = total[row]
        copies = []
        for d, peer in enumerate(z_peers):
            rows = pl.multiple_of(lax.rem(z + d + 1, NZ) * 32, 32)
            copy = remote(
                summed.at[h, pl.ds(rows, 32), :], landed.at[h, z], send_b.at[h, d], recv_b.at[h, d], peer
            )
            copy.start()
            copies.append(copy)
        landed[h, z] = summed[h, pl.ds(pl.multiple_of(z * 32, 32), 32), :]
        return copies

    lane = lax.broadcasted_iota(jnp.int32, (1, 128), 1)
    sign = jnp.where(lax.rem(lane, 2) == 0, 1.0, -1.0).astype(F32)

    def respond(h, copies):
        for copy in copies:
            copy.wait()
        total = landed[h, 0]
        for src in range(1, NZ):
            total = total + landed[h, src]
        cols = slice(h * 128, h * 128 + 128)
        for parity in range(2):
            stiff = response_ref[parity, 0, :, cols]
            friction = response_ref[parity, 1, :, cols]
            for slot in range(4):
                for c in range(2):
                    row = slot * 8 + parity * 4 + 2 * c
                    real, imag = total[row : row + 1], total[row + 1 : row + 2]
                    rows = slice((slot * 2 + c) * PAD_PERIODS, (slot * 2 + c + 1) * PAD_PERIODS)
                    for part, value in enumerate(
                        (real * stiff + imag * friction, imag * stiff - real * friction)
                    ):
                        high = value.astype(BF16)
                        left[h, parity, part, rows, 0:128] = high
                        left[h, parity, part, rows, 128:256] = (value - high.astype(F32)).astype(BF16)
                        if parity == 0 and part == 0:
                            if h == 0:
                                extra[rows, :] = value * sign
                            else:
                                extra[rows, :] += value * sign

    tile_rows = 2 * PAD_PERIODS

    def series(h, parity, part, rows, cols):
        both = left[h, parity, part, rows]
        at = slice(h * 128, h * 128 + 128)
        high, low = table_ref[parity, part, 0, at, cols], table_ref[parity, part, 1, at, cols]
        dot = functools.partial(jnp.dot, preferred_element_type=F32)
        value = dot(both, jnp.concatenate([high, high], axis=0)) + dot(both[:, :128], low)
        return value if h == 0 else value + total_series[parity, part, rows, cols]

    def add_series(h):
        def tile(index, carry):
            rows = pl.ds(pl.multiple_of(index * tile_rows, tile_rows), tile_rows)
            for col in range(HALF // 256):
                cols = slice(col * 256, col * 256 + 256)
                for parity in range(2):
                    for part in range(2):
                        total_series[parity, part, rows, cols] = series(h, parity, part, rows, cols)
            return carry

        lax.fori_loop(0, 4, tile, 0)

    def last_series(h):
        def tile(index, carry):
            rows = pl.ds(pl.multiple_of(index * tile_rows, tile_rows), tile_rows)
            most = jnp.zeros((tile_rows, 128), F32)
            for col in range(HALF // 256):
                cols = slice(col * 256, col * 256 + 256)
                cos_even, cos_odd = series(h, 0, 0, rows, cols), series(h, 1, 0, rows, cols)
                sin_even, sin_odd = series(h, 0, 1, rows, cols), series(h, 1, 1, rows, cols)
                if col == 0:
                    middle = jnp.abs(jnp.sum(extra[rows], axis=1, keepdims=True)) + jnp.abs(sin_odd[:, 0:1])
                    most = jnp.maximum(most, middle)
                    wide = lax.broadcasted_iota(jnp.int32, (1, 256), 1)
                    sin_odd = jnp.where(wide == 0, 0.0, sin_odd)
                one = jnp.abs(cos_even + cos_odd) + jnp.abs(sin_even + sin_odd)
                two = jnp.abs(cos_even - cos_odd) + jnp.abs(sin_odd - sin_even)
                peak = jnp.maximum(one, two)
                most = jnp.maximum(most, jnp.maximum(peak[:, :128], peak[:, 128:]))
            best[rows] = most
            return carry

        lax.fori_loop(0, 4, tile, 0)

    turns_each = 128 // STEPS
    first_hop, second_hop = {}, {}
    for h in range(CHUNKS):
        lax.fori_loop(h * turns_each, (h + 1) * turns_each, run, 0)
        if h == 0:
            pl.semaphore_wait(barrier, len(j_peers) + len(z_peers))
        first_hop[h] = send_parts(h)
        if h >= 1:
            second_hop[h - 1] = send_sums(h - 1, first_hop[h - 1])
        if h >= 2:
            respond(h - 2, second_hop[h - 2])
    for h in range(2):
        add_series(h)
    second_hop[3] = send_sums(3, first_hop[3])
    respond(2, second_hop[2])
    add_series(2)
    respond(3, second_hop[3])
    last_series(3)

    for slot in range(4):
        pieces = []
        for c in range(2):
            at = (slot * 2 + c) * PAD_PERIODS
            turned = jnp.transpose(jnp.concatenate([best[at : at + PAD_PERIODS], jnp.zeros((128 - PAD_PERIODS, 128), F32)], axis=0))
            pieces.append(jnp.max(turned, axis=0, keepdims=True))
        moved = pltpu.roll(pieces[1], PERIODS, 1)
        row = jnp.where(lane < PERIODS, pieces[0], moved)
        out_ref[0, slot : slot + 1, :] = row[:, : 2 * PERIODS]


def owner_peaks(inverse, fields, weights, limits, response, tables):
    dma = pltpu.SemaphoreType.DMA
    vmem = pl.BlockSpec(memory_space=pltpu.VMEM)
    return pl.pallas_call(
        peaks_kernel,
        out_shape=jax.ShapeDtypeStruct((1, 4, 2 * PERIODS), F32),
        in_specs=[pl.BlockSpec(memory_space=pltpu.SMEM)] + [vmem] * 5,
        out_specs=vmem,
        scratch_shapes=[
            pltpu.VMEM((10, OWNERS, PTS), F32),
            pltpu.VMEM((STEPS, 2 * OWNERS, PTS), BF16),
            pltpu.VMEM((STEPS, 2 * OWNERS, PTS), BF16),
            pltpu.VMEM((8 * 128, 128), F32),
            pltpu.VMEM((CHUNKS, 8, OWNERS, 128), F32),
            pltpu.VMEM((CHUNKS, NJ, 8, NZ, 128), F32),
            pltpu.VMEM((CHUNKS, NZ * 32, 128), F32),
            pltpu.VMEM((CHUNKS, NZ, 32, 128), F32),
            pltpu.VMEM((CHUNKS, 2, 2, ROWS, 256), BF16),
            pltpu.VMEM((ROWS, 128), F32),
            pltpu.VMEM((2, 2, ROWS, HALF), F32),
            pltpu.VMEM((ROWS, 128), F32),
            dma((CHUNKS, 7)), dma((CHUNKS, 7)), dma((CHUNKS, 7)), dma((CHUNKS, 7)),
        ],
        compiler_params=pltpu.CompilerParams(
            collective_id=1, has_side_effects=True, vmem_limit_bytes=48 * 2**20
        ),
        name="owner_peaks",
    )(inverse, fields, weights, limits, response, tables)


def solution(mesh):
    response, tables, inverse = constant_tables()

    def per_device(sgt, mechanism, slip_fields, rupture_start, point_count, owner_order):
        fields, weights, limits = fields_and_weights(
            sgt, mechanism, slip_fields, rupture_start, point_count, owner_order
        )
        return owner_peaks(
            jnp.asarray(inverse), fields, weights, limits, jnp.asarray(response), jnp.asarray(tables)
        )

    return jax.shard_map(
        per_device,
        mesh=mesh,
        in_specs=(
            P("site", None, None, None, "blk", None),
            P(None, "blk"),
            P("blk", None, "site"),
            P(),
            P(),
            P(),
        ),
        out_specs=P("site", "blk", None),
        check_vma=False,
    )
```

```python
import functools

import jax
import jax.numpy as jnp
import ml_dtypes
import numpy as np
from jax import lax
from jax.experimental import pallas as pl
from jax.experimental.pallas import tpu as pltpu
from jax.sharding import PartitionSpec as P

MESH = pl.DeviceIdType.MESH
FREQ = 1024
PERIODS = 44
PAD_PERIODS = 48
PTS = 128
SITES = 4
NZ = 8
NJ = 8
OWNERS = NZ * NJ
CHUNKS = 4
STEPS = 32
ROWS = 8 * PAD_PERIODS
HALF = FREQ // 2
DT = 0.1
DAMPING = 0.05
TURNS = 1.0 / (2 * FREQ * DT)
F32 = jnp.float32
BF16 = jnp.bfloat16


def split_table(table):
    high = table.astype(ml_dtypes.bfloat16)
    low = (table - high.astype(np.float64)).astype(ml_dtypes.bfloat16)
    return high, low


def constant_tables():
    freq = np.arange(FREQ)
    omega = 2 * np.pi * freq * TURNS
    factor = np.where(freq == 0, 1.0, 2.0) / FREQ
    natural = 2 * np.pi / (0.2 * 50.0 ** (np.arange(PERIODS) / (PERIODS - 1)))
    stiffness = natural[:, None] ** 2 - omega[None] ** 2
    friction = 2 * DAMPING * natural[:, None] * omega[None]
    number = np.where(freq == 0, 2.0**-10, freq)
    gain = factor[None] / number[None] * natural[:, None] ** 2 / (stiffness**2 + friction**2)
    response = np.zeros((2, 2, PAD_PERIODS, HALF), np.float32)
    for parity in range(2):
        response[parity, 0, :PERIODS] = (gain * stiffness)[:, parity::2]
        response[parity, 1, :PERIODS] = (gain * friction)[:, parity::2]
    sample = np.arange(HALF)
    tables = np.zeros((2, 2, 2, HALF, HALF), ml_dtypes.bfloat16)
    for parity in range(2):
        ids = freq[parity::2]
        angle = 2 * np.pi * ((ids[:, None] * sample[None]) % (2 * FREQ)) / (2 * FREQ)
        tables[parity, 0, 0], tables[parity, 0, 1] = split_table(np.cos(angle))
        sine = np.sin(angle)
        if parity == 1:
            sine[:, 0] = np.where(np.arange(HALF) % 2 == 0, 1.0, -1.0)
        tables[parity, 1, 0], tables[parity, 1, 1] = split_table(sine)
    return response, tables, (1.0 / number**2).astype(np.float32)


def place():
    y = lax.axis_index("site")
    b = lax.axis_index("blk")
    return y, b, lax.div(b, NJ), lax.rem(b, NJ)


def remote(src, dst, send, recv, peer):
    return pltpu.make_async_remote_copy(
        src_ref=src, dst_ref=dst, send_sem=send, recv_sem=recv, device_id=peer, device_id_type=MESH
    )


def circle(turns):
    half = (turns - jnp.floor(turns + 0.5)) * jnp.float32(np.pi)
    sq = half * half
    sine = jnp.float32(1.0 / 6227020800)
    for sign, power in ((-1, 39916800), (1, 362880), (-1, 5040), (1, 120), (-1, 6)):
        sine = sine * sq + jnp.float32(sign / power)
    sine = half + half * sq * sine
    cosine = jnp.float32(-1.0 / 87178291200)
    for sign, power in ((1, 479001600), (-1, 3628800), (1, 40320), (-1, 720), (1, 24), (-1, 2)):
        cosine = cosine * sq + jnp.float32(sign / power)
    cosine = cosine * sq + 1.0
    return 1.0 - 2.0 * sine * sine, 2.0 * sine * cosine


def kernel(
    start_ref, count_ref, order_ref, inverse_ref, slip_hbm, mech_hbm, sgt_hbm, response_hbm, table_hbm, out_ref,
    slip_ref, mech_ref, sgt, response_ref, table_ref,
    mine, plane, block, chosen, points, mech_wide, turning, weights, limits_ref, fields_ref,
    state, source_cos, source_sin, parts, arrived, summed, landed, left, extra, total_series, best,
    load_sem, send_a, recv_a, send_b, recv_b, send_c, recv_c, send_d, recv_d, send_e, recv_e,
):
    y, b, z, j = place()
    slip_load = pltpu.make_async_copy(slip_hbm, slip_ref, load_sem.at[2])
    mech_load = pltpu.make_async_copy(mech_hbm, mech_ref, load_sem.at[3])
    loads = [pltpu.make_async_copy(sgt_hbm.at[0, c], sgt.at[c], load_sem.at[c]) for c in range(2)]
    response_load = pltpu.make_async_copy(response_hbm, response_ref, load_sem.at[4])
    table_load = pltpu.make_async_copy(table_hbm, table_ref, load_sem.at[5])
    for load in (slip_load, mech_load, *loads, response_load, table_load):
        load.start()
    y_peers = [(lax.rem(y + d, SITES), b) for d in range(1, SITES)]
    j_peers = [(y, z * NJ + lax.rem(j + d, NJ)) for d in range(1, NJ)]
    z_peers = [(y, lax.rem(z + d, NZ) * NJ + j) for d in range(1, NZ)]
    turns = [(dy, dj) for dj in range(NJ) for dy in range(SITES) if dy or dj]
    plane_peers = [(lax.rem(y + dy, SITES), z * NJ + lax.rem(j + dj, NJ)) for dy, dj in turns]
    barrier = pltpu.get_barrier_semaphore()
    for peer in plane_peers + z_peers:
        pl.semaphore_signal(barrier, inc=1, device_id=peer, device_id_type=MESH)
    slip_load.wait()
    for v in range(4):
        for zz in range(2):
            for jj in range(NJ):
                at = (zz * NJ + jj) * PTS
                for k in range(3):
                    mine[v, jj, zz, k] = slip_ref[k, v : v + 1, at : at + PTS]
    pl.semaphore_wait(barrier, len(plane_peers) + len(z_peers))
    copies = []
    for d, peer in enumerate(plane_peers):
        copy = remote(
            mine.at[peer[0], lax.rem(peer[1], NJ)], plane.at[j, pl.ds(2 * y, 2)], send_a.at[d], recv_a.at[d], peer
        )
        copy.start()
        copies.append(copy)
    plane[j, pl.ds(2 * y, 2)] = mine[y, j]

    mech_load.wait()
    turned = jnp.transpose(jnp.concatenate([mech_ref[...], jnp.zeros((2, PTS), F32)], axis=0))
    for k in range(6):
        mech_wide[k] = jnp.broadcast_to(turned[:, k : k + 1], (PTS, PTS))

    def weights_of(c):
        def tile(step, carry):
            at = pl.multiple_of(step * PTS, PTS)
            for part in range(2):
                total = mech_wide[0] * sgt[c, 0, part, :, pl.ds(at, PTS)].astype(F32)
                for k in range(1, 6):
                    total = total + mech_wide[k] * sgt[c, k, part, :, pl.ds(at, PTS)].astype(F32)
                turning[part] = jnp.transpose(total)
                for parity in range(2):
                    picked = turning[part, pl.ds(parity, PTS // 2, stride=2), :]
                    for half in range(2):
                        group = step * 4 + half * 2 + parity
                        value = picked[half * 32 : half * 32 + 32]
                        same, other = slice(part * PTS, part * PTS + PTS), slice((1 - part) * PTS, (2 - part) * PTS)
                        weights[group, 64 * c : 64 * c + 32, same] = value.astype(BF16)
                        weights[group, 64 * c + 32 : 64 * c + 64, other] = (value if part else -value).astype(BF16)
            return carry

        lax.fori_loop(0, FREQ // PTS, tile, 0)

    loads[0].wait()
    weights_of(0)
    for copy in copies:
        copy.wait()
    copies = []
    for d, peer in enumerate(z_peers):
        target = lax.rem(z + d + 1, NZ)
        copy = remote(plane.at[:, target], block.at[y, z], send_b.at[d], recv_b.at[d], peer)
        copy.start()
        copies.append(copy)
    block[y, z] = plane[:, z]
    spread = []

    def forward(turn, row):
        for d, peer in enumerate(y_peers):
            copy = remote(block.at[y, row], block.at[y, row], send_c.at[turn, d], recv_c.at[turn, d], peer)
            copy.start()
            spread.append(copy)

    forward(0, z)

    def choose(row, carry):
        owner = lax.rem(row, NZ) * NJ + lax.div(row, NZ)
        best = jnp.int32(0)
        active = jnp.int32(0)
        for slot in range(4):
            v = order_ref[owner * 4 + slot]
            first = start_ref[v]
            remaining = count_ref[v] - (b - first) * PTS
            live = (first <= b) & (remaining > 0)
            best = jnp.where(live, v, best)
            active = jnp.where(live, remaining, active)
        chosen[row] = best
        points[row] = active
        return carry

    lax.fori_loop(0, OWNERS, choose, 0)
    for d, copy in enumerate(copies):
        copy.wait_recv()
        forward(d + 1, lax.rem(z + NZ - d - 1, NZ))

    def bounds(index, carry):
        slot, zz = lax.div(index, NZ), lax.rem(index, NZ)
        v = order_ref[(zz * NJ + j) * 4 + slot]
        first = start_ref[v]
        span = lax.shift_right_logical(count_ref[v] + (PTS - 1), 7)
        limits_ref[0, pl.ds(index, 1), :] = jnp.full((1, 128), first, jnp.int32)
        limits_ref[1, pl.ds(index, 1), :] = jnp.full((1, 128), first + span, jnp.int32)
        return carry

    lax.fori_loop(0, 4 * NZ, bounds, 0)
    loads[1].wait()
    weights_of(1)
    for copy in copies:
        copy.wait_send()
    for copy in spread:
        copy.wait()

    lane = lax.broadcasted_iota(jnp.int32, (1, PTS), 1)

    def select(row, carry):
        v = chosen[row]
        at = (v & 3, lax.shift_right_logical(v, 5), lax.shift_right_logical(v, 2) & 7)
        fields_ref[0, pl.ds(row, 1), :] = jnp.where(lane < points[row], block[at + (0,)], 0.0)
        fields_ref[1, pl.ds(row, 1), :] = block[at + (1,)]
        fields_ref[2, pl.ds(row, 1), :] = block[at + (2,)]
        return carry

    lax.fori_loop(0, OWNERS, select, 0)

    amp = fields_ref[0]
    turns = fields_ref[1] * jnp.float32(TURNS)
    rise = fields_ref[2] * jnp.float32(2 * np.pi * TURNS)
    one_c, one_s = circle(turns)
    state[0] = amp
    state[1] = jnp.zeros_like(amp)
    state[2] = amp * one_c
    state[3] = amp * one_s
    step_c, step_s = circle(turns * 2.0)
    state[4] = step_c
    state[5] = step_s
    state[8] = 2.0 * step_c
    jump_c, jump_s = circle(turns * jnp.float32(2 * STEPS))
    state[6] = jump_c
    state[7] = jump_s
    state[9] = rise * rise

    half_lane = lax.broadcasted_iota(jnp.int32, (OWNERS, 128), 1) & 31

    def sources_of(turn, parity):
        base = turn * (2 * STEPS) + parity
        for pair in range(OWNERS // 16):
            rows = slice(pair * 16, pair * 16 + 16)
            double = state[8, rows]
            rise_sq = state[9, rows]
            cos_now, sin_now = state[2 * parity, rows], state[2 * parity + 1, rows]
            step_c, step_s = state[4, rows], state[5, rows]
            jump_c, jump_s = state[6, rows], state[7, rows]
            state[2 * parity, rows] = cos_now * jump_c - sin_now * jump_s
            state[2 * parity + 1, rows] = sin_now * jump_c + cos_now * jump_s
            cos_next = cos_now * step_c - sin_now * step_s
            sin_next = sin_now * step_c + cos_now * step_s
            for i in range(STEPS):
                scale = lax.rsqrt(rise_sq + inverse_ref[base + 2 * i])
                source_cos[parity, i, rows, :] = (cos_now * scale).astype(BF16)
                source_sin[parity, i, rows, :] = (sin_now * scale).astype(BF16)
                if i < STEPS - 1:
                    cos_now, cos_next = cos_next, double * cos_next - cos_now
                    sin_now, sin_next = sin_next, double * sin_next - sin_now

    def sums_of(h, local, turn, parity):
        rhs = weights[turn * 2 + parity]
        total = jnp.zeros((OWNERS, 128), F32)
        for i0 in range(0, STEPS, 16):
            lhs = jnp.concatenate(
                [ref[parity, i0 : i0 + 16].reshape(16 * OWNERS, PTS) for ref in (source_cos, source_sin)], axis=1
            )
            product = lax.dot_general(lhs, rhs, (((1,), (1,)), ((), ())), preferred_element_type=F32)
            for i in range(16):
                total = jnp.where(half_lane == i0 + i, product[i * OWNERS : (i + 1) * OWNERS], total)
        parts[h, parity * 4 + local] = total

    def spectra_of(h):
        def run(local, carry):
            turn = h * 4 + local
            sums_of(h, local - 1, turn - 1, 1)
            sources_of(turn, 0)
            sums_of(h, local, turn, 0)
            sources_of(turn, 1)
            return carry

        sources_of(h * 4, 0)
        sums_of(h, 0, h * 4, 0)
        sources_of(h * 4, 1)
        lax.fori_loop(1, 4, run, 0)
        sums_of(h, 3, h * 4 + 3, 1)

    def send_parts(h):
        copies = []
        for d, peer in enumerate(j_peers):
            rows = pl.multiple_of(lax.rem(j + d + 1, NJ) * NZ, 8)
            copy = remote(
                parts.at[h, :, pl.ds(rows, NZ), :], arrived.at[h, j], send_d.at[h, d], recv_d.at[h, d], peer
            )
            copy.start()
            copies.append(copy)
        arrived[h, j] = parts[h, :, pl.ds(pl.multiple_of(j * NZ, 8), NZ), :]
        return copies

    def send_sums(h, copies):
        for copy in copies:
            copy.wait()
        for slot in range(4):
            first = limits_ref[0, slot * NZ : slot * NZ + NZ]
            last = limits_ref[1, slot * NZ : slot * NZ + NZ]
            total = jnp.zeros((8, NZ, 128), F32)
            for src in range(NJ):
                at = z * NJ + src
                live = (first <= at) & (at < last)
                total = total + jnp.where(live[None], arrived[h, src], 0.0)
            for row in range(8):
                summed[h, pl.ds(slot * 8 + row, NZ, stride=32), :] = total[row]
        copies = []
        for d, peer in enumerate(z_peers):
            rows = pl.multiple_of(lax.rem(z + d + 1, NZ) * 32, 32)
            copy = remote(
                summed.at[h, pl.ds(rows, 32), :], landed.at[h, z], send_e.at[h, d], recv_e.at[h, d], peer
            )
            copy.start()
            copies.append(copy)
        landed[h, z] = summed[h, pl.ds(pl.multiple_of(z * 32, 32), 32), :]
        return copies

    sign = jnp.where(lax.rem(lane, 2) == 0, 1.0, -1.0).astype(F32)

    def respond(h, copies):
        for copy in copies:
            copy.wait()
        total = landed[h, 0]
        for src in range(1, NZ):
            total = total + landed[h, src]
        moved = [total] + [pltpu.roll(total, 32 * d, 1) for d in range(1, 4)]
        segment = lax.shift_right_logical(lane, 5)

        def lined(first, k):
            rows = [moved[(g - k) % 4][first + g : first + g + 1] for g in range(4)]
            return jnp.where(segment < 2, jnp.where(segment < 1, rows[0], rows[1]), jnp.where(segment < 3, rows[2], rows[3]))

        cols = slice(h * 128, h * 128 + 128)
        for parity in range(2):
            stiff = response_ref[parity, 0, :, cols]
            friction = response_ref[parity, 1, :, cols]
            for slot in range(4):
                for c in range(2):
                    first = slot * 8 + parity * 4
                    real, imag = lined(first, 2 * c), lined(first, 2 * c + 1)
                    rows = slice((slot * 2 + c) * PAD_PERIODS, (slot * 2 + c + 1) * PAD_PERIODS)
                    for part, value in enumerate(
                        (real * stiff + imag * friction, imag * stiff - real * friction)
                    ):
                        high = value.astype(BF16)
                        left[h, parity, part, rows, 0:128] = high
                        left[h, parity, part, rows, 128:256] = (value - high.astype(F32)).astype(BF16)
                        if parity == 0 and part == 0:
                            if h == 0:
                                extra[rows, :] = value * sign
                            else:
                                extra[rows, :] += value * sign

    tile_rows = 2 * PAD_PERIODS

    def series(h, parity, part, rows, cols):
        both = left[h, parity, part, rows]
        at = slice(h * 128, h * 128 + 128)
        high, low = table_ref[parity, part, 0, at, cols], table_ref[parity, part, 1, at, cols]
        dot = functools.partial(jnp.dot, preferred_element_type=F32)
        value = dot(both, jnp.concatenate([high, high], axis=0)) + dot(both[:, :128], low)
        return value if h == 0 else value + total_series[parity, part, rows, cols]

    def add_series(h):
        def tile(index, carry):
            rows = pl.ds(pl.multiple_of(index * tile_rows, tile_rows), tile_rows)
            for col in range(HALF // 256):
                cols = slice(col * 256, col * 256 + 256)
                for parity in range(2):
                    for part in range(2):
                        total_series[parity, part, rows, cols] = series(h, parity, part, rows, cols)
            return carry

        lax.fori_loop(0, 4, tile, 0)

    def last_series(h):
        def tile(index, carry):
            rows = pl.ds(pl.multiple_of(index * tile_rows, tile_rows), tile_rows)
            most = jnp.zeros((tile_rows, 128), F32)
            for col in range(HALF // 256):
                cols = slice(col * 256, col * 256 + 256)
                cos_even, cos_odd = series(h, 0, 0, rows, cols), series(h, 1, 0, rows, cols)
                sin_even, sin_odd = series(h, 0, 1, rows, cols), series(h, 1, 1, rows, cols)
                if col == 0:
                    middle = jnp.abs(jnp.sum(extra[rows], axis=1, keepdims=True)) + jnp.abs(sin_odd[:, 0:1])
                    most = jnp.maximum(most, middle)
                    wide = lax.broadcasted_iota(jnp.int32, (1, 256), 1)
                    sin_odd = jnp.where(wide == 0, 0.0, sin_odd)
                one = jnp.abs(cos_even + cos_odd) + jnp.abs(sin_even + sin_odd)
                two = jnp.abs(cos_even - cos_odd) + jnp.abs(sin_odd - sin_even)
                peak = jnp.maximum(one, two)
                most = jnp.maximum(most, jnp.maximum(peak[:, :128], peak[:, 128:]))
            best[rows] = most
            return carry

        lax.fori_loop(0, 4, tile, 0)

    first_hop, second_hop = {}, {}
    for h in range(CHUNKS):
        spectra_of(h)
        first_hop[h] = send_parts(h)
        if h >= 1:
            second_hop[h - 1] = send_sums(h - 1, first_hop[h - 1])
        if h == 2:
            response_load.wait()
        if h >= 2:
            respond(h - 2, second_hop[h - 2])
    table_load.wait()
    for h in range(2):
        add_series(h)
    second_hop[3] = send_sums(3, first_hop[3])
    respond(2, second_hop[2])
    add_series(2)
    respond(3, second_hop[3])
    last_series(3)

    for slot in range(4):
        pieces = []
        for c in range(2):
            at = (slot * 2 + c) * PAD_PERIODS
            turned = jnp.transpose(jnp.concatenate([best[at : at + PAD_PERIODS], jnp.zeros((128 - PAD_PERIODS, 128), F32)], axis=0))
            pieces.append(jnp.max(turned, axis=0, keepdims=True))
        moved = pltpu.roll(pieces[1], PERIODS, 1)
        row = jnp.where(lane < PERIODS, pieces[0], moved)
        out_ref[0, slot : slot + 1, :] = row[:, : 2 * PERIODS]


def program(start, count, order, inverse, slip, mechanism, sgt, response, tables):
    dma = pltpu.SemaphoreType.DMA
    smem = pl.BlockSpec(memory_space=pltpu.SMEM)
    hbm = pl.BlockSpec(memory_space=pl.ANY)
    return pl.pallas_call(
        kernel,
        out_shape=jax.ShapeDtypeStruct((1, 4, 2 * PERIODS), F32),
        in_specs=[smem] * 4 + [hbm] * 5,
        out_specs=pl.BlockSpec(memory_space=pltpu.VMEM),
        scratch_shapes=[
            pltpu.VMEM((3, 4, 2 * NJ * PTS), F32),
            pltpu.VMEM((6, PTS), F32),
            pltpu.VMEM((2, 6, 2, PTS, FREQ), BF16),
            pltpu.VMEM(response.shape, F32),
            pltpu.VMEM(tables.shape, BF16),
            pltpu.VMEM((4, NJ, 2, 3, 1, PTS), F32),
            pltpu.VMEM((NJ, NZ, 3, 1, PTS), F32),
            pltpu.VMEM((4, NZ, NJ, 3, 1, PTS), F32),
            pltpu.SMEM((OWNERS,), jnp.int32),
            pltpu.SMEM((OWNERS,), jnp.int32),
            pltpu.VMEM((6, PTS, PTS), F32),
            pltpu.VMEM((2, PTS, PTS), F32),
            pltpu.VMEM((FREQ // 32, PTS, 2 * PTS), BF16),
            pltpu.VMEM((2, 4 * NZ, 128), jnp.int32),
            pltpu.VMEM((3, OWNERS, PTS), F32),
            pltpu.VMEM((10, OWNERS, PTS), F32),
            pltpu.VMEM((2, STEPS, OWNERS, PTS), BF16),
            pltpu.VMEM((2, STEPS, OWNERS, PTS), BF16),
            pltpu.VMEM((CHUNKS, 8, OWNERS, 128), F32),
            pltpu.VMEM((CHUNKS, NJ, 8, NZ, 128), F32),
            pltpu.VMEM((CHUNKS, NZ * 32, 128), F32),
            pltpu.VMEM((CHUNKS, NZ, 32, 128), F32),
            pltpu.VMEM((CHUNKS, 2, 2, ROWS, 256), BF16),
            pltpu.VMEM((ROWS, 128), F32),
            pltpu.VMEM((2, 2, ROWS, HALF), F32),
            pltpu.VMEM((ROWS, 128), F32),
            dma((6,)), dma((31,)), dma((31,)), dma((7,)), dma((7,)), dma((8, 3)), dma((8, 3)),
            dma((CHUNKS, 7)), dma((CHUNKS, 7)), dma((CHUNKS, 7)), dma((CHUNKS, 7)),
        ],
        compiler_params=pltpu.CompilerParams(
            collective_id=0, has_side_effects=True, vmem_limit_bytes=60 * 2**20
        ),
        name="spectral_accelerations",
    )(start, count, order, inverse, jnp.transpose(slip, (1, 0, 2)), mechanism, sgt, response, tables)


def solution(mesh):
    response, tables, inverse = constant_tables()

    def per_device(sgt, mechanism, slip_fields, rupture_start, point_count, owner_order):
        return program(
            rupture_start, point_count, owner_order, jnp.asarray(inverse), slip_fields, mechanism, sgt,
            jnp.asarray(response), jnp.asarray(tables),
        )

    return jax.shard_map(
        per_device,
        mesh=mesh,
        in_specs=(
            P("site", None, None, None, "blk", None),
            P(None, "blk"),
            P("blk", None, "site"),
            P(),
            P(),
            P(),
        ),
        out_specs=P("site", "blk", None),
        check_vma=False,
    )
```

```python
import functools

import jax
import jax.numpy as jnp
import ml_dtypes
import numpy as np
from jax import lax
from jax.experimental import pallas as pl
from jax.experimental.pallas import tpu as pltpu
from jax.sharding import PartitionSpec as P

MESH = pl.DeviceIdType.MESH
FREQ = 1024
PERIODS = 44
PAD_PERIODS = 48
PTS = 128
SITES = 4
NZ = 8
NJ = 8
OWNERS = NZ * NJ
CHUNKS = 4
STEPS = 32
ROWS = 8 * PAD_PERIODS
HALF = FREQ // 2
DT = 0.1
DAMPING = 0.05
TURNS = 1.0 / (2 * FREQ * DT)
F32 = jnp.float32
BF16 = jnp.bfloat16


def split_table(table):
    high = table.astype(ml_dtypes.bfloat16)
    low = (table - high.astype(np.float64)).astype(ml_dtypes.bfloat16)
    return high, low


def constant_tables():
    freq = np.arange(FREQ)
    omega = 2 * np.pi * freq * TURNS
    factor = np.where(freq == 0, 1.0, 2.0) / FREQ
    natural = 2 * np.pi / (0.2 * 50.0 ** (np.arange(PERIODS) / (PERIODS - 1)))
    stiffness = natural[:, None] ** 2 - omega[None] ** 2
    friction = 2 * DAMPING * natural[:, None] * omega[None]
    number = np.where(freq == 0, 2.0**-10, freq)
    gain = factor[None] / number[None] * natural[:, None] ** 2 / (stiffness**2 + friction**2)
    response = np.zeros((2, 2, PAD_PERIODS, HALF), np.float32)
    for parity in range(2):
        response[parity, 0, :PERIODS] = (gain * stiffness)[:, parity::2]
        response[parity, 1, :PERIODS] = (gain * friction)[:, parity::2]
    sample = np.arange(HALF)
    tables = np.zeros((2, 2, 2, HALF, HALF), ml_dtypes.bfloat16)
    for parity in range(2):
        ids = freq[parity::2]
        angle = 2 * np.pi * ((ids[:, None] * sample[None]) % (2 * FREQ)) / (2 * FREQ)
        tables[parity, 0, 0], tables[parity, 0, 1] = split_table(np.cos(angle))
        sine = np.sin(angle)
        if parity == 1:
            sine[:, 0] = np.where(np.arange(HALF) % 2 == 0, 1.0, -1.0)
        tables[parity, 1, 0], tables[parity, 1, 1] = split_table(sine)
    inverse = np.broadcast_to((1.0 / number**2).astype(np.float32)[:, None, None], (FREQ, 8, 128))
    return response, tables, np.ascontiguousarray(inverse)


def place():
    y = lax.axis_index("site")
    b = lax.axis_index("blk")
    return y, b, lax.div(b, NJ), lax.rem(b, NJ)


def remote(src, dst, send, recv, peer):
    return pltpu.make_async_remote_copy(
        src_ref=src, dst_ref=dst, send_sem=send, recv_sem=recv, device_id=peer, device_id_type=MESH
    )


def circle(turns):
    half = (turns - jnp.floor(turns + 0.5)) * jnp.float32(np.pi)
    sq = half * half
    sine = jnp.float32(1.0 / 6227020800)
    for sign, power in ((-1, 39916800), (1, 362880), (-1, 5040), (1, 120), (-1, 6)):
        sine = sine * sq + jnp.float32(sign / power)
    sine = half + half * sq * sine
    cosine = jnp.float32(-1.0 / 87178291200)
    for sign, power in ((1, 479001600), (-1, 3628800), (1, 40320), (-1, 720), (1, 24), (-1, 2)):
        cosine = cosine * sq + jnp.float32(sign / power)
    cosine = cosine * sq + 1.0
    return 1.0 - 2.0 * sine * sine, 2.0 * sine * cosine


def kernel(
    start_hbm, count_hbm, order_hbm, inverse_hbm, slip_hbm, mech_hbm, sgt_hbm, response_hbm, table_hbm, out_ref,
    start_ref, count_ref, order_ref, inverse_ref, slip_ref, mech_ref, sgt, response_ref, table_ref,
    mine, plane, block, chosen, points, mech_wide, turning, weights, limits_ref, fields_ref,
    state, source_cos, source_sin, parts, arrived, summed, landed, left, extra, total_series, best,
    load_sem, send_a, recv_a, send_b, recv_b, send_c, recv_c, send_d, recv_d, send_e, recv_e,
):
    y, b, z, j = place()
    slip_load = pltpu.make_async_copy(slip_hbm, slip_ref, load_sem.at[2])
    mech_load = pltpu.make_async_copy(mech_hbm, mech_ref, load_sem.at[3])
    loads = [pltpu.make_async_copy(sgt_hbm.at[0, c], sgt.at[c], load_sem.at[c]) for c in range(2)]
    response_load = pltpu.make_async_copy(response_hbm, response_ref, load_sem.at[4])
    table_load = pltpu.make_async_copy(table_hbm, table_ref, load_sem.at[5])
    index_loads = [
        pltpu.make_async_copy(src, dst, load_sem.at[6 + k])
        for k, (src, dst) in enumerate(
            ((start_hbm, start_ref), (count_hbm, count_ref), (order_hbm, order_ref))
        )
    ]
    inverse_load = pltpu.make_async_copy(inverse_hbm, inverse_ref, load_sem.at[9])
    for load in (slip_load, mech_load, *loads, *index_loads, inverse_load, response_load, table_load):
        load.start()
    y_peers = [(lax.rem(y + d, SITES), b) for d in range(1, SITES)]
    j_peers = [(y, z * NJ + lax.rem(j + d, NJ)) for d in range(1, NJ)]
    z_peers = [(y, lax.rem(z + d, NZ) * NJ + j) for d in range(1, NZ)]
    turns = [(dy, dj) for dj in range(NJ) for dy in range(SITES) if dy or dj]
    plane_peers = [(lax.rem(y + dy, SITES), z * NJ + lax.rem(j + dj, NJ)) for dy, dj in turns]
    barrier = pltpu.get_barrier_semaphore()
    for peer in plane_peers + z_peers:
        pl.semaphore_signal(barrier, inc=1, device_id=peer, device_id_type=MESH)
    slip_load.wait()
    for v in range(4):
        for zz in range(2):
            for jj in range(NJ):
                at = (zz * NJ + jj) * PTS
                for k in range(3):
                    mine[v, jj, zz, k] = slip_ref[k, v : v + 1, at : at + PTS]
    pl.semaphore_wait(barrier, len(plane_peers) + len(z_peers))
    copies = []
    for d, peer in enumerate(plane_peers):
        copy = remote(
            mine.at[peer[0], lax.rem(peer[1], NJ)], plane.at[j, pl.ds(2 * y, 2)], send_a.at[d], recv_a.at[d], peer
        )
        copy.start()
        copies.append(copy)
    plane[j, pl.ds(2 * y, 2)] = mine[y, j]

    mech_load.wait()
    turned = jnp.transpose(jnp.concatenate([mech_ref[...], jnp.zeros((2, PTS), F32)], axis=0))
    for k in range(6):
        mech_wide[k] = jnp.broadcast_to(turned[:, k : k + 1], (PTS, PTS))

    def weights_of(c):
        def tile(step, carry):
            at = pl.multiple_of(step * PTS, PTS)
            for part in range(2):
                total = mech_wide[0] * sgt[c, 0, part, :, pl.ds(at, PTS)].astype(F32)
                for k in range(1, 6):
                    total = total + mech_wide[k] * sgt[c, k, part, :, pl.ds(at, PTS)].astype(F32)
                turning[part] = jnp.transpose(total)
                for parity in range(2):
                    picked = turning[part, pl.ds(parity, PTS // 2, stride=2), :]
                    for half in range(2):
                        group = step * 4 + half * 2 + parity
                        value = picked[half * 32 : half * 32 + 32]
                        same, other = slice(part * PTS, part * PTS + PTS), slice((1 - part) * PTS, (2 - part) * PTS)
                        weights[group, 64 * c : 64 * c + 32, same] = value.astype(BF16)
                        weights[group, 64 * c + 32 : 64 * c + 64, other] = (value if part else -value).astype(BF16)
            return carry

        lax.fori_loop(0, FREQ // PTS, tile, 0)

    loads[0].wait()
    weights_of(0)
    for copy in copies:
        copy.wait()
    copies = []
    for d, peer in enumerate(z_peers):
        target = lax.rem(z + d + 1, NZ)
        copy = remote(plane.at[:, target], block.at[y, z], send_b.at[d], recv_b.at[d], peer)
        copy.start()
        copies.append(copy)
    block[y, z] = plane[:, z]
    spread = []

    def forward(turn, row):
        for d, peer in enumerate(y_peers):
            copy = remote(block.at[y, row], block.at[y, row], send_c.at[turn, d], recv_c.at[turn, d], peer)
            copy.start()
            spread.append(copy)

    forward(0, z)

    for load in index_loads:
        load.wait()

    def choose(row, carry):
        owner = lax.rem(row, NZ) * NJ + lax.div(row, NZ)
        best = jnp.int32(0)
        active = jnp.int32(0)
        for slot in range(4):
            v = order_ref[owner * 4 + slot]
            first = start_ref[v]
            remaining = count_ref[v] - (b - first) * PTS
            live = (first <= b) & (remaining > 0)
            best = jnp.where(live, v, best)
            active = jnp.where(live, remaining, active)
        chosen[row] = best
        points[row] = active
        return carry

    lax.fori_loop(0, OWNERS, choose, 0)
    for d, copy in enumerate(copies):
        copy.wait_recv()
        forward(d + 1, lax.rem(z + NZ - d - 1, NZ))

    def bounds(index, carry):
        slot, zz = lax.div(index, NZ), lax.rem(index, NZ)
        v = order_ref[(zz * NJ + j) * 4 + slot]
        first = start_ref[v]
        span = lax.shift_right_logical(count_ref[v] + (PTS - 1), 7)
        limits_ref[0, pl.ds(index, 1), :] = jnp.full((1, 128), first, jnp.int32)
        limits_ref[1, pl.ds(index, 1), :] = jnp.full((1, 128), first + span, jnp.int32)
        return carry

    lax.fori_loop(0, 4 * NZ, bounds, 0)
    loads[1].wait()
    weights_of(1)
    for copy in copies:
        copy.wait_send()
    for copy in spread:
        copy.wait()

    lane = lax.broadcasted_iota(jnp.int32, (1, PTS), 1)

    def select(row, carry):
        v = chosen[row]
        at = (v & 3, lax.shift_right_logical(v, 5), lax.shift_right_logical(v, 2) & 7)
        fields_ref[0, pl.ds(row, 1), :] = jnp.where(lane < points[row], block[at + (0,)], 0.0)
        fields_ref[1, pl.ds(row, 1), :] = block[at + (1,)]
        fields_ref[2, pl.ds(row, 1), :] = block[at + (2,)]
        return carry

    lax.fori_loop(0, OWNERS, select, 0)

    amp = fields_ref[0]
    turns = fields_ref[1] * jnp.float32(TURNS)
    rise = fields_ref[2] * jnp.float32(2 * np.pi * TURNS)
    one_c, one_s = circle(turns)
    state[0] = amp
    state[1] = jnp.zeros_like(amp)
    state[2] = amp * one_c
    state[3] = amp * one_s
    step_c, step_s = circle(turns * 2.0)
    state[4] = step_c
    state[5] = step_s
    state[8] = 2.0 * step_c
    jump_c, jump_s = circle(turns * jnp.float32(2 * STEPS))
    state[6] = jump_c
    state[7] = jump_s
    state[9] = rise * rise

    half_lane = lax.broadcasted_iota(jnp.int32, (8, 128), 1) & 31

    def sources_of(turn, parity):
        base = turn * (2 * STEPS) + parity
        for pair in range(OWNERS // 16):
            rows = slice(pair * 16, pair * 16 + 16)
            double = state[8, rows]
            rise_sq = state[9, rows]
            cos_now, sin_now = state[2 * parity, rows], state[2 * parity + 1, rows]
            step_c, step_s = state[4, rows], state[5, rows]
            jump_c, jump_s = state[6, rows], state[7, rows]
            state[2 * parity, rows] = cos_now * jump_c - sin_now * jump_s
            state[2 * parity + 1, rows] = sin_now * jump_c + cos_now * jump_s
            cos_next = cos_now * step_c - sin_now * step_s
            sin_next = sin_now * step_c + cos_now * step_s
            for i in range(STEPS):
                inverse = inverse_ref[base + 2 * i]
                scale = lax.rsqrt(rise_sq + jnp.concatenate([inverse, inverse], axis=0))
                source_cos[parity, i, rows, :] = (cos_now * scale).astype(BF16)
                source_sin[parity, i, rows, :] = (sin_now * scale).astype(BF16)
                if i < STEPS - 1:
                    cos_now, cos_next = cos_next, double * cos_next - cos_now
                    sin_now, sin_next = sin_next, double * sin_next - sin_now

    def sums_of(turn, parity):
        rhs = weights[turn * 2 + parity]
        total = None
        for i0 in range(0, STEPS, 16):
            lhs = jnp.concatenate(
                [ref[parity, i0 : i0 + 16].reshape(16 * OWNERS, PTS) for ref in (source_cos, source_sin)], axis=1
            )
            product = lax.dot_general(lhs, rhs, (((1,), (1,)), ((), ())), preferred_element_type=F32)
            for i in range(16):
                rows = [product[i * OWNERS + k * 8 : i * OWNERS + k * 8 + 8] for k in range(OWNERS // 8)]
                if total is None:
                    total = rows
                else:
                    own = half_lane == i0 + i
                    total = [jnp.where(own, new, old) for new, old in zip(rows, total)]
        for k in range(OWNERS // 8):
            parts[turn * 2 + parity, k * 8 : k * 8 + 8] = total[k]

    def turn_of(turn, carry):
        sums_of(turn - 1, 1)
        sources_of(turn, 0)
        sums_of(turn, 0)
        sources_of(turn, 1)
        return carry

    pieces = [(0, 8), (8, 8), (16, 4), (20, 4), (24, 4), (28, 4)]

    def send_parts(index):
        at, size = pieces[index]
        groups = pl.ds(at, size)
        copies = []
        for d, peer in enumerate(j_peers):
            rows = pl.multiple_of(lax.rem(j + d + 1, NJ) * NZ, 8)
            copy = remote(
                parts.at[groups, pl.ds(rows, NZ), :], arrived.at[j, groups], send_d.at[index, d], recv_d.at[index, d], peer
            )
            copy.start()
            copies.append(copy)
        arrived[j, groups] = parts[groups, pl.ds(pl.multiple_of(j * NZ, 8), NZ), :]
        return copies

    def send_sums(index, copies):
        at, size = pieces[index]
        for copy in copies:
            copy.wait()
        for slot in range(4):
            first = limits_ref[0, slot * NZ : slot * NZ + NZ]
            last = limits_ref[1, slot * NZ : slot * NZ + NZ]
            total = jnp.zeros((size, NZ, 128), F32)
            for src in range(NJ):
                block_id = z * NJ + src
                live = (first <= block_id) & (block_id < last)
                total = total + jnp.where(live[None], arrived[src, at : at + size], 0.0)
            for row in range(size):
                summed[pl.ds(at * 32 + slot * size + row, NZ, stride=4 * size), :] = total[row]
        copies = []
        for d, peer in enumerate(z_peers):
            rows = pl.multiple_of(at * 32 + lax.rem(z + d + 1, NZ) * (4 * size), 8)
            copy = remote(
                summed.at[pl.ds(rows, 4 * size), :], landed.at[z, pl.ds(4 * at, 4 * size)],
                send_e.at[index, d], recv_e.at[index, d], peer,
            )
            copy.start()
            copies.append(copy)
        landed[z, pl.ds(4 * at, 4 * size)] = summed[pl.ds(pl.multiple_of(at * 32 + z * (4 * size), 8), 4 * size), :]
        return copies

    sign = jnp.where(lax.rem(lane, 2) == 0, 1.0, -1.0).astype(F32)

    def respond(h, copies):
        for copy in copies:
            copy.wait()
        total = landed[0, h * 32 : h * 32 + 32]
        for src in range(1, NZ):
            total = total + landed[src, h * 32 : h * 32 + 32]
        size = 8 if h < 2 else 4
        moved = [total] + [pltpu.roll(total, 32 * d, 1) for d in range(1, 4)]
        segment = lax.shift_right_logical(lane, 5)

        def lined(slot, parity, k):
            rows = []
            for g in range(4):
                group = g * 2 + parity
                row = group // size * 4 * size + slot * size + group % size
                rows.append(moved[(g - k) % 4][row : row + 1])
            return jnp.where(segment < 2, jnp.where(segment < 1, rows[0], rows[1]), jnp.where(segment < 3, rows[2], rows[3]))

        cols = slice(h * 128, h * 128 + 128)
        for parity in range(2):
            stiff = response_ref[parity, 0, :, cols]
            friction = response_ref[parity, 1, :, cols]
            for slot in range(4):
                for c in range(2):
                    real, imag = lined(slot, parity, 2 * c), lined(slot, parity, 2 * c + 1)
                    rows = slice((slot * 2 + c) * PAD_PERIODS, (slot * 2 + c + 1) * PAD_PERIODS)
                    for part, value in enumerate(
                        (real * stiff + imag * friction, imag * stiff - real * friction)
                    ):
                        high = value.astype(BF16)
                        left[h, parity, part, rows, 0:128] = high
                        left[h, parity, part, rows, 128:256] = (value - high.astype(F32)).astype(BF16)
                        if parity == 0 and part == 0:
                            if h == 0:
                                extra[rows, :] = value * sign
                            else:
                                extra[rows, :] += value * sign

    tile_rows = 2 * PAD_PERIODS

    def series(h, parity, part, rows, cols):
        both = left[h, parity, part, rows]
        at = slice(h * 128, h * 128 + 128)
        high, low = table_ref[parity, part, 0, at, cols], table_ref[parity, part, 1, at, cols]
        dot = functools.partial(jnp.dot, preferred_element_type=F32)
        value = dot(both, jnp.concatenate([high, high], axis=0)) + dot(both[:, :128], low)
        return value if h == 0 else value + total_series[parity, part, rows, cols]

    def add_series(h):
        def tile(index, carry):
            rows = pl.ds(pl.multiple_of(index * tile_rows, tile_rows), tile_rows)
            for col in range(HALF // 256):
                cols = slice(col * 256, col * 256 + 256)
                for parity in range(2):
                    for part in range(2):
                        total_series[parity, part, rows, cols] = series(h, parity, part, rows, cols)
            return carry

        lax.fori_loop(0, 4, tile, 0)

    def last_series(h):
        def tile(index, carry):
            rows = pl.ds(pl.multiple_of(index * tile_rows, tile_rows), tile_rows)
            most = jnp.zeros((tile_rows, 128), F32)
            for col in range(HALF // 256):
                cols = slice(col * 256, col * 256 + 256)
                cos_even, cos_odd = series(h, 0, 0, rows, cols), series(h, 1, 0, rows, cols)
                sin_even, sin_odd = series(h, 0, 1, rows, cols), series(h, 1, 1, rows, cols)
                if col == 0:
                    middle = jnp.abs(jnp.sum(extra[rows], axis=1, keepdims=True)) + jnp.abs(sin_odd[:, 0:1])
                    most = jnp.maximum(most, middle)
                    wide = lax.broadcasted_iota(jnp.int32, (1, 256), 1)
                    sin_odd = jnp.where(wide == 0, 0.0, sin_odd)
                one = jnp.abs(cos_even + cos_odd) + jnp.abs(sin_even + sin_odd)
                two = jnp.abs(cos_even - cos_odd) + jnp.abs(sin_odd - sin_even)
                peak = jnp.maximum(one, two)
                most = jnp.maximum(most, jnp.maximum(peak[:, :128], peak[:, 128:]))
            best[rows] = most
            return carry

        lax.fori_loop(0, 4, tile, 0)

    first_hop, second_hop = {}, {}
    inverse_load.wait()
    sources_of(0, 0)
    sums_of(0, 0)
    sources_of(0, 1)
    lax.fori_loop(1, 5, turn_of, 0)
    first_hop[0] = send_parts(0)
    lax.fori_loop(5, 9, turn_of, 0)
    first_hop[1] = send_parts(1)
    second_hop[0] = send_sums(0, first_hop[0])
    lax.fori_loop(9, 11, turn_of, 0)
    first_hop[2] = send_parts(2)
    lax.fori_loop(11, 13, turn_of, 0)
    first_hop[3] = send_parts(3)
    second_hop[1] = send_sums(1, first_hop[1])
    response_load.wait()
    respond(0, second_hop[0])
    lax.fori_loop(13, 15, turn_of, 0)
    first_hop[4] = send_parts(4)
    second_hop[2] = send_sums(2, first_hop[2])
    lax.fori_loop(15, 16, turn_of, 0)
    sums_of(15, 1)
    first_hop[5] = send_parts(5)
    second_hop[3] = send_sums(3, first_hop[3])
    second_hop[4] = send_sums(4, first_hop[4])
    respond(1, second_hop[1])
    table_load.wait()
    add_series(0)
    second_hop[5] = send_sums(5, first_hop[5])
    add_series(1)
    respond(2, second_hop[2] + second_hop[3])
    add_series(2)
    respond(3, second_hop[4] + second_hop[5])
    last_series(3)

    turned = [jnp.transpose(best[at : at + 128]) for at in range(0, ROWS, 128)]
    peaks = [jnp.max(value, axis=0, keepdims=True) for value in turned]

    def placed(first, lanes):
        at, offset = divmod(first, 128)
        shift = (lanes - offset) % 128
        moved = [pltpu.roll(value, shift, 1) if shift else value for value in peaks[at : at + 2]]
        if offset + PERIODS <= 128:
            return moved[0]
        return jnp.where(lane < lanes + 128 - offset, moved[0], moved[1])

    for slot in range(4):
        first = slot * 2 * PAD_PERIODS
        row = jnp.where(lane < PERIODS, placed(first, 0), placed(first + PAD_PERIODS, PERIODS))
        out_ref[0, slot : slot + 1, :] = row[:, : 2 * PERIODS]


def program(start, count, order, inverse, slip, mechanism, sgt, response, tables):
    dma = pltpu.SemaphoreType.DMA
    hbm = pl.BlockSpec(memory_space=pl.ANY)
    return pl.pallas_call(
        kernel,
        out_shape=jax.ShapeDtypeStruct((1, 4, 2 * PERIODS), F32),
        in_specs=[hbm] * 9,
        out_specs=pl.BlockSpec(memory_space=pltpu.VMEM),
        scratch_shapes=[
            pltpu.SMEM(start.shape, jnp.int32),
            pltpu.SMEM(count.shape, jnp.int32),
            pltpu.SMEM(order.shape, jnp.int32),
            pltpu.VMEM(inverse.shape, F32),
            pltpu.VMEM((3, 4, 2 * NJ * PTS), F32),
            pltpu.VMEM((6, PTS), F32),
            pltpu.VMEM((2, 6, 2, PTS, FREQ), BF16),
            pltpu.VMEM(response.shape, F32),
            pltpu.VMEM(tables.shape, BF16),
            pltpu.VMEM((4, NJ, 2, 3, 1, PTS), F32),
            pltpu.VMEM((NJ, NZ, 3, 1, PTS), F32),
            pltpu.VMEM((4, NZ, NJ, 3, 1, PTS), F32),
            pltpu.SMEM((OWNERS,), jnp.int32),
            pltpu.SMEM((OWNERS,), jnp.int32),
            pltpu.VMEM((6, PTS, PTS), F32),
            pltpu.VMEM((2, PTS, PTS), F32),
            pltpu.VMEM((FREQ // 32, PTS, 2 * PTS), BF16),
            pltpu.VMEM((2, 4 * NZ, 128), jnp.int32),
            pltpu.VMEM((3, OWNERS, PTS), F32),
            pltpu.VMEM((10, OWNERS, PTS), F32),
            pltpu.VMEM((2, STEPS, OWNERS, PTS), BF16),
            pltpu.VMEM((2, STEPS, OWNERS, PTS), BF16),
            pltpu.VMEM((FREQ // 32, OWNERS, 128), F32),
            pltpu.VMEM((NJ, FREQ // 32, NZ, 128), F32),
            pltpu.VMEM((FREQ // 32 * 4 * NZ, 128), F32),
            pltpu.VMEM((NZ, FREQ // 32 * 4, 128), F32),
            pltpu.VMEM((CHUNKS, 2, 2, ROWS, 256), BF16),
            pltpu.VMEM((ROWS, 128), F32),
            pltpu.VMEM((2, 2, ROWS, HALF), F32),
            pltpu.VMEM((ROWS, 128), F32),
            dma((10,)), dma((31,)), dma((31,)), dma((7,)), dma((7,)), dma((8, 3)), dma((8, 3)),
            dma((6, 7)), dma((6, 7)), dma((6, 7)), dma((6, 7)),
        ],
        compiler_params=pltpu.CompilerParams(
            collective_id=0, has_side_effects=True, vmem_limit_bytes=60 * 2**20
        ),
        name="spectral_accelerations",
    )(start, count, order, inverse, jnp.transpose(slip, (1, 0, 2)), mechanism, sgt, response, tables)


def solution(mesh):
    response, tables, inverse = constant_tables()

    def per_device(sgt, mechanism, slip_fields, rupture_start, point_count, owner_order):
        return program(
            rupture_start, point_count, owner_order, jnp.asarray(inverse), slip_fields, mechanism, sgt,
            jnp.asarray(response), jnp.asarray(tables),
        )

    return jax.shard_map(
        per_device,
        mesh=mesh,
        in_specs=(
            P("site", None, None, None, "blk", None),
            P(None, "blk"),
            P("blk", None, "site"),
            P(),
            P(),
            P(),
        ),
        out_specs=P("site", "blk", None),
        check_vma=False,
    )
```

```python
import functools

import jax
import jax.numpy as jnp
import ml_dtypes
import numpy as np
from jax import lax
from jax.experimental import pallas as pl
from jax.experimental.pallas import tpu as pltpu
from jax.sharding import PartitionSpec as P

MESH = pl.DeviceIdType.MESH
FREQ = 1024
PERIODS = 44
PAD_PERIODS = 48
PTS = 128
SITES = 4
NZ = 8
NJ = 8
OWNERS = NZ * NJ
CHUNKS = 4
STEPS = 32
ROWS = 8 * PAD_PERIODS
HALF = FREQ // 2
DT = 0.1
DAMPING = 0.05
TURNS = 1.0 / (2 * FREQ * DT)
F32 = jnp.float32
BF16 = jnp.bfloat16


def split_table(table):
    high = table.astype(ml_dtypes.bfloat16)
    low = (table - high.astype(np.float64)).astype(ml_dtypes.bfloat16)
    return high, low


def constant_tables():
    freq = np.arange(FREQ)
    omega = 2 * np.pi * freq * TURNS
    factor = np.where(freq == 0, 1.0, 2.0) / FREQ
    natural = 2 * np.pi / (0.2 * 50.0 ** (np.arange(PERIODS) / (PERIODS - 1)))
    stiffness = natural[:, None] ** 2 - omega[None] ** 2
    friction = 2 * DAMPING * natural[:, None] * omega[None]
    number = np.where(freq == 0, 2.0**-10, freq)
    gain = factor[None] / number[None] * natural[:, None] ** 2 / (stiffness**2 + friction**2)
    response = np.zeros((2, 2, PAD_PERIODS, HALF), np.float32)
    for parity in range(2):
        response[parity, 0, :PERIODS] = (gain * stiffness)[:, parity::2]
        response[parity, 1, :PERIODS] = (gain * friction)[:, parity::2]
    sample = np.arange(HALF)
    tables = np.zeros((2, 2, 2, HALF, HALF), ml_dtypes.bfloat16)
    for parity in range(2):
        ids = freq[parity::2]
        angle = 2 * np.pi * ((ids[:, None] * sample[None]) % (2 * FREQ)) / (2 * FREQ)
        tables[parity, 0, 0], tables[parity, 0, 1] = split_table(np.cos(angle))
        sine = np.sin(angle)
        if parity == 1:
            sine[:, 0] = np.where(np.arange(HALF) % 2 == 0, 1.0, -1.0)
        tables[parity, 1, 0], tables[parity, 1, 1] = split_table(sine)
    inverse = np.broadcast_to((1.0 / number**2).astype(np.float32)[:, None, None], (FREQ, 8, 128))
    return response, tables, np.ascontiguousarray(inverse)


def place():
    y = lax.axis_index("site")
    b = lax.axis_index("blk")
    return y, b, lax.div(b, NJ), lax.rem(b, NJ)


def remote(src, dst, send, recv, peer):
    return pltpu.make_async_remote_copy(
        src_ref=src, dst_ref=dst, send_sem=send, recv_sem=recv, device_id=peer, device_id_type=MESH
    )


def circle(turns):
    half = (turns - jnp.floor(turns + 0.5)) * jnp.float32(np.pi)
    sq = half * half
    sine = jnp.float32(1.0 / 6227020800)
    for sign, power in ((-1, 39916800), (1, 362880), (-1, 5040), (1, 120), (-1, 6)):
        sine = sine * sq + jnp.float32(sign / power)
    sine = half + half * sq * sine
    cosine = jnp.float32(-1.0 / 87178291200)
    for sign, power in ((1, 479001600), (-1, 3628800), (1, 40320), (-1, 720), (1, 24), (-1, 2)):
        cosine = cosine * sq + jnp.float32(sign / power)
    cosine = cosine * sq + 1.0
    return 1.0 - 2.0 * sine * sine, 2.0 * sine * cosine


def kernel(
    start_hbm, count_hbm, order_hbm, inverse_hbm, slip_hbm, mech_hbm, sgt_hbm, response_hbm, table_hbm, out_ref,
    start_ref, count_ref, order_ref, inverse_ref, slip_ref, mech_ref, sgt, response_ref, table_ref,
    mine, plane, block, chosen, points, mech_wide, turning, weights, limits_ref, fields_ref,
    state, source_cos, source_sin, parts, arrived, summed, landed, left, extra, total_series, best,
    load_sem, send_a, recv_a, send_b, recv_b, send_c, recv_c, send_d, recv_d, send_e, recv_e,
):
    y, b, z, j = place()
    slip_load = pltpu.make_async_copy(slip_hbm, slip_ref, load_sem.at[2])
    mech_load = pltpu.make_async_copy(mech_hbm, mech_ref, load_sem.at[3])
    loads = [pltpu.make_async_copy(sgt_hbm.at[0, c], sgt.at[c], load_sem.at[c]) for c in range(2)]
    response_load = pltpu.make_async_copy(response_hbm, response_ref, load_sem.at[4])
    table_load = pltpu.make_async_copy(table_hbm, table_ref, load_sem.at[5])
    index_loads = [
        pltpu.make_async_copy(src, dst, load_sem.at[6 + k])
        for k, (src, dst) in enumerate(
            ((start_hbm, start_ref), (count_hbm, count_ref), (order_hbm, order_ref))
        )
    ]
    inverse_load = pltpu.make_async_copy(inverse_hbm, inverse_ref, load_sem.at[9])
    for load in (slip_load, mech_load, *loads, *index_loads, inverse_load, response_load, table_load):
        load.start()
    y_peers = [(lax.rem(y + d, SITES), b) for d in range(1, SITES)]
    j_peers = [(y, z * NJ + lax.rem(j + d, NJ)) for d in range(1, NJ)]
    z_peers = [(y, lax.rem(z + d, NZ) * NJ + j) for d in range(1, NZ)]
    turns = [(dy, dj) for dj in range(NJ) for dy in range(SITES) if dy or dj]
    plane_peers = [(lax.rem(y + dy, SITES), z * NJ + lax.rem(j + dj, NJ)) for dy, dj in turns]
    barrier = pltpu.get_barrier_semaphore()
    for peer in plane_peers + z_peers:
        pl.semaphore_signal(barrier, inc=1, device_id=peer, device_id_type=MESH)
    slip_load.wait()
    for v in range(4):
        for zz in range(2):
            for jj in range(NJ):
                at = (zz * NJ + jj) * PTS
                for k in range(3):
                    mine[v, jj, zz, k] = slip_ref[k, v : v + 1, at : at + PTS]
    pl.semaphore_wait(barrier, len(plane_peers) + len(z_peers))
    copies = []
    for d, peer in enumerate(plane_peers):
        copy = remote(
            mine.at[peer[0], lax.rem(peer[1], NJ)], plane.at[j, pl.ds(2 * y, 2)], send_a.at[d], recv_a.at[d], peer
        )
        copy.start()
        copies.append(copy)
    plane[j, pl.ds(2 * y, 2)] = mine[y, j]

    mech_load.wait()
    turned = jnp.transpose(jnp.concatenate([mech_ref[...], jnp.zeros((2, PTS), F32)], axis=0))
    for k in range(6):
        mech_wide[k] = jnp.broadcast_to(turned[:, k : k + 1], (PTS, PTS))

    def weights_of(c):
        def tile(step, carry):
            at = pl.multiple_of(step * PTS, PTS)
            for part in range(2):
                total = mech_wide[0] * sgt[c, 0, part, :, pl.ds(at, PTS)].astype(F32)
                for k in range(1, 6):
                    total = total + mech_wide[k] * sgt[c, k, part, :, pl.ds(at, PTS)].astype(F32)
                turning[part] = jnp.transpose(total)
                for parity in range(2):
                    picked = turning[part, pl.ds(parity, PTS // 2, stride=2), :]
                    for half in range(2):
                        group = step * 4 + half * 2 + parity
                        value = picked[half * 32 : half * 32 + 32]
                        same, other = slice(part * PTS, part * PTS + PTS), slice((1 - part) * PTS, (2 - part) * PTS)
                        weights[group, 64 * c : 64 * c + 32, same] = value.astype(BF16)
                        weights[group, 64 * c + 32 : 64 * c + 64, other] = (value if part else -value).astype(BF16)
            return carry

        lax.fori_loop(0, FREQ // PTS, tile, 0)

    loads[0].wait()
    weights_of(0)
    for load in index_loads:
        load.wait()

    def choose(row, carry):
        owner = lax.rem(row, NZ) * NJ + lax.div(row, NZ)
        best = jnp.int32(0)
        active = jnp.int32(0)
        for slot in range(4):
            v = order_ref[owner * 4 + slot]
            first = start_ref[v]
            remaining = count_ref[v] - (b - first) * PTS
            live = (first <= b) & (remaining > 0)
            best = jnp.where(live, v, best)
            active = jnp.where(live, remaining, active)
        chosen[row] = best
        points[row] = active
        return carry

    lax.fori_loop(0, OWNERS, choose, 0)
    for copy in copies:
        copy.wait()
    copies = []
    for d, peer in enumerate(z_peers):
        target = lax.rem(z + d + 1, NZ)
        copy = remote(plane.at[:, target], block.at[y, z], send_b.at[d], recv_b.at[d], peer)
        copy.start()
        copies.append(copy)
    block[y, z] = plane[:, z]
    spread = []

    def forward(turn, row):
        for d, peer in enumerate(y_peers):
            copy = remote(block.at[y, row], block.at[y, row], send_c.at[turn, d], recv_c.at[turn, d], peer)
            copy.start()
            spread.append(copy)

    forward(0, z)

    for d, copy in enumerate(copies):
        copy.wait_recv()
        forward(d + 1, lax.rem(z + NZ - d - 1, NZ))

    def bounds(index, carry):
        slot, zz = lax.div(index, NZ), lax.rem(index, NZ)
        v = order_ref[(zz * NJ + j) * 4 + slot]
        first = start_ref[v]
        span = lax.shift_right_logical(count_ref[v] + (PTS - 1), 7)
        limits_ref[0, pl.ds(index, 1), :] = jnp.full((1, 128), first, jnp.int32)
        limits_ref[1, pl.ds(index, 1), :] = jnp.full((1, 128), first + span, jnp.int32)
        return carry

    lax.fori_loop(0, 4 * NZ, bounds, 0)
    loads[1].wait()
    weights_of(1)
    for copy in copies:
        copy.wait_send()
    for copy in spread:
        copy.wait()

    lane = lax.broadcasted_iota(jnp.int32, (1, PTS), 1)

    def select(row, carry):
        v = chosen[row]
        at = (v & 3, lax.shift_right_logical(v, 5), lax.shift_right_logical(v, 2) & 7)
        fields_ref[0, pl.ds(row, 1), :] = jnp.where(lane < points[row], block[at + (0,)], 0.0)
        fields_ref[1, pl.ds(row, 1), :] = block[at + (1,)]
        fields_ref[2, pl.ds(row, 1), :] = block[at + (2,)]
        return carry

    lax.fori_loop(0, OWNERS, select, 0, unroll=8)

    amp = fields_ref[0]
    turns = fields_ref[1] * jnp.float32(TURNS)
    rise = fields_ref[2] * jnp.float32(2 * np.pi * TURNS)
    one_c, one_s = circle(turns)
    state[0] = amp
    state[1] = jnp.zeros_like(amp)
    state[2] = amp * one_c
    state[3] = amp * one_s
    step_c, step_s = circle(turns * 2.0)
    state[4] = step_c
    state[5] = step_s
    state[8] = 2.0 * step_c
    jump_c, jump_s = circle(turns * jnp.float32(2 * STEPS))
    state[6] = jump_c
    state[7] = jump_s
    state[9] = rise * rise

    half_lane = lax.broadcasted_iota(jnp.int32, (8, 128), 1) & 31

    def sources_of(turn, parity):
        base = turn * (2 * STEPS) + parity
        for pair in range(OWNERS // 16):
            rows = slice(pair * 16, pair * 16 + 16)
            double = state[8, rows]
            rise_sq = state[9, rows]
            cos_now, sin_now = state[2 * parity, rows], state[2 * parity + 1, rows]
            step_c, step_s = state[4, rows], state[5, rows]
            jump_c, jump_s = state[6, rows], state[7, rows]
            state[2 * parity, rows] = cos_now * jump_c - sin_now * jump_s
            state[2 * parity + 1, rows] = sin_now * jump_c + cos_now * jump_s
            cos_next = cos_now * step_c - sin_now * step_s
            sin_next = sin_now * step_c + cos_now * step_s
            for i in range(STEPS):
                inverse = inverse_ref[base + 2 * i]
                scale = lax.rsqrt(rise_sq + jnp.concatenate([inverse, inverse], axis=0))
                source_cos[parity, i, rows, :] = (cos_now * scale).astype(BF16)
                source_sin[parity, i, rows, :] = (sin_now * scale).astype(BF16)
                if i < STEPS - 1:
                    cos_now, cos_next = cos_next, double * cos_next - cos_now
                    sin_now, sin_next = sin_next, double * sin_next - sin_now

    def sums_of(turn, parity):
        rhs = weights[turn * 2 + parity]
        total = None
        for i0 in range(0, STEPS, 16):
            lhs = jnp.concatenate(
                [ref[parity, i0 : i0 + 16].reshape(16 * OWNERS, PTS) for ref in (source_cos, source_sin)], axis=1
            )
            product = lax.dot_general(lhs, rhs, (((1,), (1,)), ((), ())), preferred_element_type=F32)
            for i in range(16):
                rows = [product[i * OWNERS + k * 8 : i * OWNERS + k * 8 + 8] for k in range(OWNERS // 8)]
                if total is None:
                    total = rows
                else:
                    own = half_lane == i0 + i
                    total = [jnp.where(own, new, old) for new, old in zip(rows, total)]
        for k in range(OWNERS // 8):
            parts[turn * 2 + parity, k * 8 : k * 8 + 8] = total[k]

    def turn_of(turn, carry):
        sums_of(turn - 1, 1)
        sources_of(turn, 0)
        sums_of(turn, 0)
        sources_of(turn, 1)
        return carry

    pieces = [(0, 8), (8, 8), (16, 4), (20, 4), (24, 4), (28, 2), (30, 2)]

    def send_parts(index):
        at, size = pieces[index]
        groups = pl.ds(at, size)
        copies = []
        for d, peer in enumerate(j_peers):
            rows = pl.multiple_of(lax.rem(j + d + 1, NJ) * NZ, 8)
            copy = remote(
                parts.at[groups, pl.ds(rows, NZ), :], arrived.at[j, groups], send_d.at[index, d], recv_d.at[index, d], peer
            )
            copy.start()
            copies.append(copy)
        arrived[j, groups] = parts[groups, pl.ds(pl.multiple_of(j * NZ, 8), NZ), :]
        return copies

    def send_sums(index, copies):
        at, size = pieces[index]
        for copy in copies:
            copy.wait()
        for slot in range(4):
            first = limits_ref[0, slot * NZ : slot * NZ + NZ]
            last = limits_ref[1, slot * NZ : slot * NZ + NZ]
            total = jnp.zeros((size, NZ, 128), F32)
            for src in range(NJ):
                block_id = z * NJ + src
                live = (first <= block_id) & (block_id < last)
                total = total + jnp.where(live[None], arrived[src, at : at + size], 0.0)
            for row in range(size):
                summed[pl.ds(at * 32 + slot * size + row, NZ, stride=4 * size), :] = total[row]
        copies = []
        for d, peer in enumerate(z_peers):
            rows = pl.multiple_of(at * 32 + lax.rem(z + d + 1, NZ) * (4 * size), 8)
            copy = remote(
                summed.at[pl.ds(rows, 4 * size), :], landed.at[z, pl.ds(4 * at, 4 * size)],
                send_e.at[index, d], recv_e.at[index, d], peer,
            )
            copy.start()
            copies.append(copy)
        landed[z, pl.ds(4 * at, 4 * size)] = summed[pl.ds(pl.multiple_of(at * 32 + z * (4 * size), 8), 4 * size), :]
        return copies

    sign = jnp.where(lax.rem(lane, 2) == 0, 1.0, -1.0).astype(F32)

    def respond(h, copies):
        for copy in copies:
            copy.wait()
        total = landed[0, h * 32 : h * 32 + 32]
        for src in range(1, NZ):
            total = total + landed[src, h * 32 : h * 32 + 32]
        moved = [total] + [pltpu.roll(total, 32 * d, 1) for d in range(1, 4)]
        segment = lax.shift_right_logical(lane, 5)

        def lined(slot, parity, k):
            rows = []
            for g in range(4):
                group = g * 2 + parity
                at, size = next(p for p in pieces if p[0] <= 8 * h + group < p[0] + p[1])
                row = 4 * (at - 8 * h) + slot * size + 8 * h + group - at
                rows.append(moved[(g - k) % 4][row : row + 1])
            return jnp.where(segment < 2, jnp.where(segment < 1, rows[0], rows[1]), jnp.where(segment < 3, rows[2], rows[3]))

        cols = slice(h * 128, h * 128 + 128)
        for parity in range(2):
            stiff = response_ref[parity, 0, :, cols]
            friction = response_ref[parity, 1, :, cols]
            for slot in range(4):
                for c in range(2):
                    real, imag = lined(slot, parity, 2 * c), lined(slot, parity, 2 * c + 1)
                    rows = slice((slot * 2 + c) * PAD_PERIODS, (slot * 2 + c + 1) * PAD_PERIODS)
                    for part, value in enumerate(
                        (real * stiff + imag * friction, imag * stiff - real * friction)
                    ):
                        high = value.astype(BF16)
                        left[h, parity, part, rows, 0:128] = high
                        left[h, parity, part, rows, 128:256] = (value - high.astype(F32)).astype(BF16)
                        if parity == 0 and part == 0:
                            if h == 0:
                                extra[rows, :] = value * sign
                            else:
                                extra[rows, :] += value * sign

    tile_rows = 2 * PAD_PERIODS

    def series(h, parity, part, rows, cols):
        both = left[h, parity, part, rows]
        at = slice(h * 128, h * 128 + 128)
        high, low = table_ref[parity, part, 0, at, cols], table_ref[parity, part, 1, at, cols]
        dot = functools.partial(jnp.dot, preferred_element_type=F32)
        value = dot(both, jnp.concatenate([high, high], axis=0)) + dot(both[:, :128], low)
        return value if h == 0 else value + total_series[parity, part, rows, cols]

    def add_series(h):
        def tile(index, carry):
            rows = pl.ds(pl.multiple_of(index * tile_rows, tile_rows), tile_rows)
            for col in range(HALF // 256):
                cols = slice(col * 256, col * 256 + 256)
                for parity in range(2):
                    for part in range(2):
                        total_series[parity, part, rows, cols] = series(h, parity, part, rows, cols)
            return carry

        lax.fori_loop(0, 4, tile, 0)

    def last_series(h):
        def tile(index, carry):
            rows = pl.ds(pl.multiple_of(index * tile_rows, tile_rows), tile_rows)
            most = jnp.zeros((tile_rows, 128), F32)
            for col in range(HALF // 256):
                cols = slice(col * 256, col * 256 + 256)
                cos_even, cos_odd = series(h, 0, 0, rows, cols), series(h, 1, 0, rows, cols)
                sin_even, sin_odd = series(h, 0, 1, rows, cols), series(h, 1, 1, rows, cols)
                if col == 0:
                    middle = jnp.abs(jnp.sum(extra[rows], axis=1, keepdims=True)) + jnp.abs(sin_odd[:, 0:1])
                    most = jnp.maximum(most, middle)
                    wide = lax.broadcasted_iota(jnp.int32, (1, 256), 1)
                    sin_odd = jnp.where(wide == 0, 0.0, sin_odd)
                one = jnp.abs(cos_even + cos_odd) + jnp.abs(sin_even + sin_odd)
                two = jnp.abs(cos_even - cos_odd) + jnp.abs(sin_odd - sin_even)
                peak = jnp.maximum(one, two)
                most = jnp.maximum(most, jnp.maximum(peak[:, :128], peak[:, 128:]))
            best[rows] = most
            return carry

        lax.fori_loop(0, 4, tile, 0, unroll=2)

    first_hop, second_hop = {}, {}
    inverse_load.wait()
    sources_of(0, 0)
    sums_of(0, 0)
    sources_of(0, 1)
    lax.fori_loop(1, 5, turn_of, 0)
    first_hop[0] = send_parts(0)
    lax.fori_loop(5, 9, turn_of, 0)
    first_hop[1] = send_parts(1)
    second_hop[0] = send_sums(0, first_hop[0])
    lax.fori_loop(9, 11, turn_of, 0)
    first_hop[2] = send_parts(2)
    lax.fori_loop(11, 13, turn_of, 0)
    first_hop[3] = send_parts(3)
    second_hop[1] = send_sums(1, first_hop[1])
    response_load.wait()
    respond(0, second_hop[0])
    lax.fori_loop(13, 15, turn_of, 0)
    first_hop[4] = send_parts(4)
    second_hop[2] = send_sums(2, first_hop[2])
    sums_of(14, 1)
    sources_of(15, 0)
    first_hop[5] = send_parts(5)
    sums_of(15, 0)
    sources_of(15, 1)
    sums_of(15, 1)
    first_hop[6] = send_parts(6)
    second_hop[3] = send_sums(3, first_hop[3])
    second_hop[4] = send_sums(4, first_hop[4])
    respond(1, second_hop[1])
    table_load.wait()
    add_series(0)
    second_hop[5] = send_sums(5, first_hop[5])
    second_hop[6] = send_sums(6, first_hop[6])
    add_series(1)
    respond(2, second_hop[2] + second_hop[3])
    add_series(2)
    respond(3, second_hop[4] + second_hop[5] + second_hop[6])
    last_series(3)

    turned = [jnp.transpose(best[at : at + 128]) for at in range(0, ROWS, 128)]
    peaks = [jnp.max(value, axis=0, keepdims=True) for value in turned]

    def placed(first, lanes):
        at, offset = divmod(first, 128)
        shift = (lanes - offset) % 128
        moved = [pltpu.roll(value, shift, 1) if shift else value for value in peaks[at : at + 2]]
        if offset + PERIODS <= 128:
            return moved[0]
        return jnp.where(lane < lanes + 128 - offset, moved[0], moved[1])

    for slot in range(4):
        first = slot * 2 * PAD_PERIODS
        row = jnp.where(lane < PERIODS, placed(first, 0), placed(first + PAD_PERIODS, PERIODS))
        out_ref[0, slot : slot + 1, :] = row[:, : 2 * PERIODS]


def program(start, count, order, inverse, slip, mechanism, sgt, response, tables):
    dma = pltpu.SemaphoreType.DMA
    hbm = pl.BlockSpec(memory_space=pl.ANY)
    return pl.pallas_call(
        kernel,
        out_shape=jax.ShapeDtypeStruct((1, 4, 2 * PERIODS), F32),
        in_specs=[hbm] * 9,
        out_specs=pl.BlockSpec(memory_space=pltpu.VMEM),
        scratch_shapes=[
            pltpu.SMEM(start.shape, jnp.int32),
            pltpu.SMEM(count.shape, jnp.int32),
            pltpu.SMEM(order.shape, jnp.int32),
            pltpu.VMEM(inverse.shape, F32),
            pltpu.VMEM((3, 4, 2 * NJ * PTS), F32),
            pltpu.VMEM((6, PTS), F32),
            pltpu.VMEM((2, 6, 2, PTS, FREQ), BF16),
            pltpu.VMEM(response.shape, F32),
            pltpu.VMEM(tables.shape, BF16),
            pltpu.VMEM((4, NJ, 2, 3, 1, PTS), F32),
            pltpu.VMEM((NJ, NZ, 3, 1, PTS), F32),
            pltpu.VMEM((4, NZ, NJ, 3, 1, PTS), F32),
            pltpu.SMEM((OWNERS,), jnp.int32),
            pltpu.SMEM((OWNERS,), jnp.int32),
            pltpu.VMEM((6, PTS, PTS), F32),
            pltpu.VMEM((2, PTS, PTS), F32),
            pltpu.VMEM((FREQ // 32, PTS, 2 * PTS), BF16),
            pltpu.VMEM((2, 4 * NZ, 128), jnp.int32),
            pltpu.VMEM((3, OWNERS, PTS), F32),
            pltpu.VMEM((10, OWNERS, PTS), F32),
            pltpu.VMEM((2, STEPS, OWNERS, PTS), BF16),
            pltpu.VMEM((2, STEPS, OWNERS, PTS), BF16),
            pltpu.VMEM((FREQ // 32, OWNERS, 128), F32),
            pltpu.VMEM((NJ, FREQ // 32, NZ, 128), F32),
            pltpu.VMEM((FREQ // 32 * 4 * NZ, 128), F32),
            pltpu.VMEM((NZ, FREQ // 32 * 4, 128), F32),
            pltpu.VMEM((CHUNKS, 2, 2, ROWS, 256), BF16),
            pltpu.VMEM((ROWS, 128), F32),
            pltpu.VMEM((2, 2, ROWS, HALF), F32),
            pltpu.VMEM((ROWS, 128), F32),
            dma((10,)), dma((31,)), dma((31,)), dma((7,)), dma((7,)), dma((8, 3)), dma((8, 3)),
            dma((7, 7)), dma((7, 7)), dma((7, 7)), dma((7, 7)),
        ],
        compiler_params=pltpu.CompilerParams(
            collective_id=0, has_side_effects=True, vmem_limit_bytes=60 * 2**20
        ),
        name="spectral_accelerations",
    )(start, count, order, inverse, jnp.transpose(slip, (1, 0, 2)), mechanism, sgt, response, tables)


def solution(mesh):
    response, tables, inverse = constant_tables()

    def per_device(sgt, mechanism, slip_fields, rupture_start, point_count, owner_order):
        return program(
            rupture_start, point_count, owner_order, jnp.asarray(inverse), slip_fields, mechanism, sgt,
            jnp.asarray(response), jnp.asarray(tables),
        )

    return jax.shard_map(
        per_device,
        mesh=mesh,
        in_specs=(
            P("site", None, None, None, "blk", None),
            P(None, "blk"),
            P("blk", None, "site"),
            P(),
            P(),
            P(),
        ),
        out_specs=P("site", "blk", None),
        check_vma=False,
    )
```
